128 devices in a mesh: gx: 8 (over x, core), gy: 16 (over z, y).
Axes of the slice: x: 4, y: 4, z: 4, core: 2. Of those that a mesh axis runs over, the one named last changes fastest.
Arguments:
- multipoles: bfloat16 [32768, 121], P(('gx', 'gy')), may hold values from -6 to 6
- m2l_ops: bfloat16 [316, 121, 121], replicated, may hold values from -0.0625 to 0.0625
- want_boxes: int32 [128, 16, 128], P(('gx', 'gy')), may hold values from 0 to 255
- m2l_source: int32 [32768, 189], P(('gx', 'gy')), may hold values from 0 to 2303, as said below
- m2l_offset: int32 [32768, 189], P(('gx', 'gy')), may hold values from 0 to 315, as said below
- m2l_count: int32 [32768], P(('gx', 'gy')), may hold values from 1 to 189, as said below
- positions: float32 [32768, 3, 128], P(('gx', 'gy')), may hold values from 0 to 1
- charges: float32 [32768, 128], P(('gx', 'gy')), may hold values from -6 to 6
- part_count: int32 [32768], P(('gx', 'gy')), may hold values from 1 to 128
- pair_target: int32 [128, 1024], P(('gx', 'gy')), may hold values from 0 to 255
- pair_source: int32 [128, 1024], P(('gx', 'gy')), may hold values from 0 to 511, as said below
- pair_offset: int32 [128, 1024], P(('gx', 'gy')), may hold values from 0 to 26, as said below
- pair_count: int32 [128], P(('gx', 'gy')), may hold values from 1 to 1024, as said below
Outputs:
- local_exp: float32 [32768, 121], P(('gx', 'gy'))
- near_field: float32 [32768, 128], P(('gx', 'gy'))
The draws below stay inside these ranges and needn't reach their ends.
Inputs may be any that keep to these rules, and one draw needn't show every extreme that they name: `m2l_offset`: the 189 offset numbers of one box are distinct. Slots k >= m2l_count[t] of a box's interaction list are unused. `m2l_source`: an entry of box t on device d that names reach n has 0 <= d + rel(n) < 0 + number of devices, so only devices inside the mesh are named. Slots k >= pair_count[d] of device d are unused. `pair_source`: on the last device every entry is below 256. `pair_offset`: never 13.
All inputs are finite; a program needn't handle non-finite values.
Results may differ from the reference program's by a relative error of at most 0.0003.
Values may be sent and summed in bfloat16 or wider, within the bound.
No kernel may reach another device: no remote copies, remote signals or barrier semaphores. Data moves between devices by JAX's collectives and lax.ppermute only.
A program may use at most 128 MiB of HBM per device.

```python
import jax
import jax.numpy as jnp
from jax import lax

COEF = 121
OFFS = 316
KMAX = 189
PB = 128
NEAR = 16
BOX_DEV = 256
CAP = 128
PAIR_DEV = 1024
BOXES = 32768
SLOTS = 2048
DEVICES = 128


def device_levels(key):
    return jax.random.randint(key, (BOXES // BOX_DEV,), 1, 4)


def draw_m2l_count(key, part):
    levels = device_levels(key)
    key = jax.random.fold_in(key, 3)
    first_key, second_key = jax.random.split(key)
    ceiling = jnp.repeat(levels * KMAX // 3, BOX_DEV)
    counts = 1 + jax.random.randint(first_key, (BOXES,), 0, 1 << 20) % ceiling
    chosen = jax.random.randint(second_key, (), 0, BOXES)
    return jnp.where(jnp.arange(BOXES) == chosen, KMAX, counts).astype(jnp.int32)


def draw_pair_count(key, part):
    levels = device_levels(key)
    key = jax.random.fold_in(key, 7)
    first_key, second_key = jax.random.split(key)
    device_count = BOXES // BOX_DEV
    ceiling = levels * PAIR_DEV // 3
    counts = 1 + jax.random.randint(first_key, (device_count,), 0, 1 << 20) % ceiling
    chosen = jax.random.randint(second_key, (), 0, device_count)
    return jnp.where(jnp.arange(device_count) == chosen, PAIR_DEV, counts).astype(jnp.int32)


def draw_m2l_source(key, part):
    key = jax.random.fold_in(key, 15)
    device_count = BOXES // BOX_DEV
    half = NEAR // 2
    raw_ids = jax.random.randint(key, (BOXES, KMAX), 0, BOX_DEV + SLOTS)
    device_ids = (jnp.arange(BOXES, dtype=jnp.int32) // BOX_DEV)[:, None]
    rest = jnp.maximum(raw_ids - BOX_DEV, 0)
    reach = rest // CAP
    within = rest % CAP
    relative = reach - half + (reach >= half).astype(jnp.int32)
    inside = (device_ids + relative >= 0) & (device_ids + relative < device_count)
    mirrored = BOX_DEV + (NEAR - 1 - reach) * CAP + within
    fixed = jnp.where(inside, raw_ids, mirrored)
    return jnp.where(raw_ids < BOX_DEV, raw_ids, fixed).astype(jnp.int32)


def draw_m2l_offset(key, part):
    key = jax.random.fold_in(key, 5)
    scores = jax.random.randint(key, (BOXES, OFFS), 0, 1 << 20) * OFFS + jnp.arange(OFFS)[None, :]
    order = jnp.argsort(scores, axis=1)
    return order[:, :KMAX].astype(jnp.int32)


def draw_part_count(key, part):
    key = jax.random.fold_in(key, 9)
    first_key, second_key = jax.random.split(key)
    counts = 1 + jax.random.randint(first_key, (BOXES,), 0, PB)
    chosen = jax.random.randint(second_key, (), 0, BOXES)
    return jnp.where(jnp.arange(BOXES) == chosen, PB, counts).astype(jnp.int32)


def draw_pair_source(key, part):
    key = jax.random.fold_in(key, 11)
    device_count = BOXES // BOX_DEV
    raw_ids = jax.random.randint(key, (device_count, PAIR_DEV), 0, 2 * BOX_DEV)
    last_row = jnp.arange(device_count)[:, None] == device_count - 1
    return jnp.where(last_row, raw_ids % BOX_DEV, raw_ids).astype(jnp.int32)


def draw_pair_offset(key, part):
    key = jax.random.fold_in(key, 13)
    raw_ids = jax.random.randint(key, (BOXES // BOX_DEV, PAIR_DEV), 0, 26)
    return (raw_ids + (raw_ids >= 13).astype(jnp.int32)).astype(jnp.int32)


def place_ends(result, key, smallest, high):
    extent = result.shape
    index_at = [jax.random.randint(jax.random.fold_in(key, axis), (), 0, extent[axis]) for axis in range(len(extent))]
    result = result.at[tuple(index_at)].set(smallest)
    longest = extent.index(max(extent))
    index_at[longest] = (index_at[longest] + 1) % extent[longest]
    return result.at[tuple(index_at)].set(high)


def level_of(key, extent, cuts, least, largest):
    gain, own = 1.0, jax.random.fold_in(key, 6)
    for dim, shards_of in cuts:
        heights = jnp.exp(jax.random.uniform(jax.random.fold_in(own, dim), (shards_of,), jnp.float32, least / len(cuts), largest / len(cuts)))
        gain = gain * jnp.repeat(heights, extent[dim] // shards_of).reshape([-1 if axis == dim else 1 for axis in range(len(extent))])
    return gain


def centred(stream_key, shape, width, most, cuts=(), held_as=jnp.bfloat16):
    drawn = width * jax.random.normal(stream_key, shape, jnp.float32)
    if cuts:
        drawn = drawn * level_of(stream_key, shape, cuts, -0.22, 0.18)
    return jnp.clip(drawn, -most, most).astype(held_as)


def setup_inputs(seed: int = 0) -> dict:
    seeds = jax.random.split(jax.random.key(seed), 14)
    multipoles = centred(seeds[0], (BOXES, COEF), 1.0, 6.0, ((0, 128),))
    m2l_ops = centred(seeds[1], (OFFS, COEF, COEF), (COEF * KMAX // 3) ** -0.5, 0.0625)
    want_boxes = place_ends(jax.random.randint(seeds[2], (DEVICES, NEAR, CAP), 0, BOX_DEV), jax.random.fold_in(seeds[2], 1), 0, BOX_DEV - 1).astype(jnp.int32)
    m2l_source = draw_m2l_source(jax.random.fold_in(seeds[13], 71), 0)
    m2l_offset = draw_m2l_offset(jax.random.fold_in(seeds[13], 71), 0)
    m2l_count = draw_m2l_count(jax.random.fold_in(seeds[13], 71), 0)
    positions = jnp.clip(1.0 * jax.random.uniform(seeds[6], (BOXES, 3, PB), jnp.float32) ** level_of(seeds[6], (BOXES, 3, PB), ((0, 128),), -0.2, 0.2), 0.0, 1.0)
    charges = centred(seeds[7], (BOXES, PB), 1.0, 6.0, ((0, 128),), jnp.float32)
    part_count = draw_part_count(jax.random.fold_in(seeds[13], 71), 0)
    pair_target = place_ends(jax.random.randint(seeds[9], (DEVICES, PAIR_DEV), 0, BOX_DEV), jax.random.fold_in(seeds[9], 1), 0, BOX_DEV - 1).astype(jnp.int32)
    pair_source = draw_pair_source(jax.random.fold_in(seeds[13], 71), 0)
    pair_offset = draw_pair_offset(jax.random.fold_in(seeds[13], 71), 0)
    pair_count = draw_pair_count(jax.random.fold_in(seeds[13], 71), 0)
    return {"multipoles": multipoles, "m2l_ops": m2l_ops, "want_boxes": want_boxes, "m2l_source": m2l_source, "m2l_offset": m2l_offset, "m2l_count": m2l_count, "positions": positions, "charges": charges, "part_count": part_count, "pair_target": pair_target, "pair_source": pair_source, "pair_offset": pair_offset, "pair_count": pair_count}


SOFTEN = 0.05

def offset_vectors(offset):
    return jnp.stack([offset // 9 - 1, offset // 3 % 3 - 1, offset % 3 - 1], axis=-1).astype(jnp.float32)

def kernel_block(target_pos, source_pos, displace):
    total = jnp.full((target_pos.shape[0], target_pos.shape[2], source_pos.shape[2]), SOFTEN * SOFTEN, jnp.float32)
    for component in range(3):
        spread = target_pos[:, component, :, None] - source_pos[:, component, None, :] - displace[:, component, None, None]
        total = total + spread * spread
    return 1.0 / jnp.sqrt(total)

def reference(multipoles, m2l_ops, want_boxes, m2l_source, m2l_offset, m2l_count, positions, charges, part_count, pair_target, pair_source, pair_offset, pair_count):
    device_count = BOXES // BOX_DEV
    half = NEAR // 2
    reach_ids = jnp.arange(NEAR, dtype=jnp.int32)
    relative = reach_ids - half + (reach_ids >= half).astype(jnp.int32)
    peers = jnp.clip(jnp.arange(device_count, dtype=jnp.int32)[:, None] + relative[None, :], 0, device_count - 1)
    remote = (peers[:, :, None] * BOX_DEV + want_boxes).reshape(device_count, SLOTS)
    own_ids = jnp.arange(device_count, dtype=jnp.int32)[:, None] * BOX_DEV + jnp.arange(BOX_DEV, dtype=jnp.int32)[None, :]
    lookup = jnp.concatenate([own_ids, remote], axis=1).reshape(-1)
    box_ids = jnp.arange(BOXES, dtype=jnp.int32)
    source_box = jnp.take(lookup, (box_ids // BOX_DEV)[:, None] * (BOX_DEV + SLOTS) + m2l_source)
    ops_flat = m2l_ops.astype(jnp.float32).reshape(OFFS * COEF, COEF)
    widened = multipoles.astype(jnp.float32)

    def expand(pieces):
        source_ids, offset_ids, counts = pieces
        used = jnp.arange(KMAX, dtype=jnp.int32)[None, :] < counts[:, None]
        gathered = jnp.where(used[:, :, None], jnp.take(widened, source_ids, axis=0), 0.0)
        dense = jnp.zeros((BOX_DEV, OFFS, COEF), jnp.float32).at[jnp.arange(BOX_DEV, dtype=jnp.int32)[:, None], offset_ids].add(gathered)
        return jnp.dot(dense.reshape(BOX_DEV, OFFS * COEF), ops_flat, precision=lax.Precision.HIGHEST)
    local_exp = lax.map(expand, (source_box.reshape(-1, BOX_DEV, KMAX), m2l_offset.reshape(-1, BOX_DEV, KMAX), m2l_count.reshape(-1, BOX_DEV))).reshape(BOXES, COEF)
    live_slot = jnp.arange(PB, dtype=jnp.int32)[None, :] < part_count[:, None]
    charges_live = jnp.where(live_slot, charges, 0.0)
    base = (jnp.arange(device_count, dtype=jnp.int32) * BOX_DEV)[:, None]
    global_target = (base + pair_target).reshape(-1)
    global_source = (base + pair_source).reshape(-1)
    used_pair = (jnp.arange(PAIR_DEV, dtype=jnp.int32)[None, :] < pair_count[:, None]).reshape(-1)
    pair_block = min(128, PAIR_DEV)

    def pair_one(pieces):
        target_ids, source_ids, offset_ids, usable = pieces
        kern = kernel_block(jnp.take(positions, target_ids, axis=0), jnp.take(positions, source_ids, axis=0), offset_vectors(offset_ids))
        weight = usable.astype(jnp.float32)[:, None]
        at_target = lax.optimization_barrier(jnp.sum(kern * jnp.take(charges_live, source_ids, axis=0)[:, None, :], axis=2)) * weight
        at_source = lax.optimization_barrier(jnp.sum(kern * jnp.take(charges_live, target_ids, axis=0)[:, :, None], axis=1)) * weight
        return (at_target, at_source)
    at_target, at_source = lax.map(pair_one, (global_target.reshape(-1, pair_block), global_source.reshape(-1, pair_block), pair_offset.reshape(-1, pair_block), used_pair.reshape(-1, pair_block)))
    pair_field = jax.ops.segment_sum(at_target.reshape(-1, PB), global_target, num_segments=BOXES)
    pair_field = pair_field + jax.ops.segment_sum(at_source.reshape(-1, PB), global_source, num_segments=BOXES)
    diagonal = jnp.arange(PB)[:, None] == jnp.arange(PB)[None, :]

    def self_one(pieces):
        block_pos, block_q = pieces
        kern = kernel_block(block_pos, block_pos, jnp.zeros((block_pos.shape[0], 3), jnp.float32))
        kern = jnp.where(diagonal[None], 0.0, kern)
        return lax.optimization_barrier(jnp.sum(kern * block_q[:, None, :], axis=2))
    self_field = lax.map(self_one, (positions.reshape(-1, BOX_DEV, 3, PB), charges_live.reshape(-1, BOX_DEV, PB))).reshape(BOXES, PB)
    near_field = jnp.where(live_slot, self_field + pair_field, 0.0)
    return (local_exp, near_field)
```

```python
import functools

import jax
import jax.numpy as jnp
from jax import lax
from jax.experimental import pallas as pl
from jax.experimental.pallas import tpu as pltpu
from jax.sharding import PartitionSpec as P

BOX, PB, EPS = 256, 128, 0.0025
OFFS, OP, KMAX, KP, COEF, NEAR, CAP = 316, 320, 189, 192, 121, 16, 128
ZROW = BOX + NEAR * CAP
NTAB = ZROW + 8
f32, bf16 = jnp.float32, jnp.bfloat16
AXES = ("gx", "gy")

def split3(v):
    a=v.astype(bf16).astype(f32); r=v-a
    b=r.astype(bf16).astype(f32); c=r-b
    return a,b,c

def near_body(U,PU,tgt_ref,src_ref,off_ref,cnt_ref,own_ref,nxt_ref,tcol_ref,srow_ref,out_ref,fwd_ref,xb,fa,qa,cc,dd,vv):
    sub=lax.broadcasted_iota(jnp.int32,(8,128),0)
    m3=(sub<3).astype(f32)
    one=jnp.ones((8,128),f32); zero=jnp.zeros((8,128),f32)
    for o in range(27):
        v=(o//9-1,(o//3)%3-1,o%3-1)
        vv[o]=jnp.where(sub==0,float(v[0]),jnp.where(sub==1,float(v[1]),jnp.where(sub==2,float(v[2]),0.0)))
    def rows(g,_):
        for half,ref in ((0,own_ref),(1,nxt_ref)):
            for c in range(4):
                p=ref[c,pl.ds(pl.multiple_of(g*8,8),8),:]
                if c<3: p=p-0.5
                xb[pl.ds(half*BOX*8+g*64+c,8,stride=8),:]=p
            for c in range(4,8):
                xb[pl.ds(half*BOX*8+g*64+c,8,stride=8),:]=zero
        return 0
    lax.fori_loop(0,BOX//8,rows,0)
    def feat_b(y):
        y1,y2,y3=split3(y)
        q1,q2,q3=split3(y*y)
        return jnp.concatenate([y1,y1,y1,y2,y2,y3,q1,q2,q3,one]+[zero]*6,0).astype(bf16)
    diag=lax.broadcasted_iota(jnp.int32,(PB,PB),0)==lax.broadcasted_iota(jnp.int32,(PB,PB),1)
    def sq(b):
        return xb[pl.ds(pl.multiple_of(b*8,8),8),:]
    def prep(g,_):
        for u in range(PU):
            b=g*PU+u
            x=sq(b)
            x1,x2,x3=split3(x*-2.0)
            xm=x*m3
            s=jnp.sum(xm*xm,axis=0,keepdims=True)+EPS
            s=jnp.broadcast_to(s,(8,128))
            s1,s2,s3=split3(s)
            sr=jnp.where(sub==0,s1,jnp.where(sub==1,s2,jnp.where(sub==2,s3,0.0)))
            x1,x2,x3=x1*m3,x2*m3,x3*m3
            f=jnp.concatenate([x1,x2,x3,x1,x2,x1,m3,m3,m3,sr,x]+[zero]*5,0)
            t=f.T
            ft=jnp.where(lax.broadcasted_iota(jnp.int32,(PB,128),1)<80,t,0.0).astype(bf16)
            fa[b]=ft
            q=jnp.broadcast_to(t[:,83:84],(PB,PB))
            qa[b]=q
            k=lax.rsqrt(jnp.dot(ft,feat_b(x),preferred_element_type=f32))
            k=jnp.where(diag,0.0,k)
            out_ref[pl.ds(b,1),:]=jnp.sum(k*q,axis=0,keepdims=True)
        return 0
    lax.fori_loop(0,BOX//PU,prep,0)
    n=cnt_ref[0]
    def zinit(i,_):
        dd[pl.ds(pl.multiple_of(i*8,8),8),:]=zero
        cc[pl.ds(pl.multiple_of(i*8,8),8),:]=zero
        return 0
    lax.fori_loop(0,128,zinit,0)
    lane=lax.broadcasted_iota(jnp.int32,(PB,128),1)
    if True:
        def pairs(g,_):
            cs=[]
            for u in range(U):
                p=g*U+u
                a=tgt_ref[p]; b=src_ref[p]; o=off_ref[p]
                y=sq(b)+vv[o]
                k=lax.rsqrt(jnp.dot(fa[a],feat_b(y),preferred_element_type=f32))
                qb=xb[pl.ds(b*8+3,1),:]
                dd[pl.ds(p,1),:]=jnp.sum(k*qa[a],axis=0,keepdims=True)
                cs.append(jnp.sum(k*qb,axis=1,keepdims=True))
            blk=lax.shift_right_logical(g*U,7)
            l0=(g*U)&127
            r=pl.ds(pl.multiple_of(blk*128,128),128)
            c=cc[r,:]
            for u in range(U):
                c=jnp.where(lane==l0+u,cs[u],c)
            cc[r,:]=c
            return 0
        lax.fori_loop(0,lax.div(n+U-1,U),pairs,0)
    fwd_ref[...]=jnp.zeros_like(fwd_ref)
    def scat(k,_):
        r=pl.ds(pl.multiple_of(k*128,128),128)
        prow=k*128+lax.broadcasted_iota(jnp.int32,(1,128),1)
        tid=jnp.where(prow<n,tcol_ref[pl.ds(k,1),:],-1)
        sid=jnp.where(prow<n,srow_ref[pl.ds(k,1),:],-1)
        oh_t=(lax.broadcasted_iota(jnp.int32,(BOX,128),0)==tid).astype(f32).astype(bf16)
        oh_s=(lax.broadcasted_iota(jnp.int32,(2*BOX,128),0)==sid).astype(f32).astype(bf16)
        c1,c2,c3=split3(cc[r,:])
        d1,d2,d3=split3(dd[r,:])
        nt=(((1,),(1,)),((),()))
        ct=sum(lax.dot_general(oh_t,c.astype(bf16),nt,preferred_element_type=f32) for c in (c1,c2,c3))
        ds=sum(jnp.dot(oh_s,d.astype(bf16),preferred_element_type=f32) for d in (d1,d2,d3))
        out_ref[...]+=ct+ds[:BOX]
        fwd_ref[...]+=ds[BOX:]
        return 0
    lax.fori_loop(0,lax.div(n+127,128),scat,0)

def near(tgt,src,off,cnt,own4,nxt4,U=32,PU=8):
    sm=pl.BlockSpec(memory_space=pltpu.SMEM); vm=pl.BlockSpec(memory_space=pltpu.VMEM)
    return pl.pallas_call(functools.partial(near_body,U,PU),
        out_shape=(jax.ShapeDtypeStruct((BOX,PB),f32),jax.ShapeDtypeStruct((BOX,PB),f32)),
        in_specs=[sm]*4+[vm]*4,
        out_specs=(vm,vm),
        scratch_shapes=[pltpu.VMEM((2*BOX*8,128),f32),pltpu.VMEM((BOX,PB,128),bf16),pltpu.VMEM((BOX,PB,128),f32),
            pltpu.VMEM((1024,128),f32),pltpu.VMEM((1024,128),f32),pltpu.VMEM((27,8,128),f32)],
        compiler_params=pltpu.CompilerParams(vmem_limit_bytes=56<<20),
        name="near")(tgt,src,off,cnt,own4,nxt4,tgt.reshape(8,128),src.reshape(8,128))

def relayout_body(in_ref,out_ref,buf):
    OB=in_ref.shape[1]
    buf[...]=jnp.zeros_like(buf)
    for c in range(COEF):
        buf[c*OB:(c+1)*OB,:COEF]=in_ref[c].astype(f32)
    for o in range(OB):
        out_ref[o]=buf[pl.ds(o,128,stride=OB),:].astype(bf16)

def relayout(ops_t,OB=32):
    return pl.pallas_call(relayout_body,
        out_shape=jax.ShapeDtypeStruct((OP,128,128),bf16),
        grid=(OP//OB,),
        in_specs=[pl.BlockSpec((COEF,OB,COEF),lambda i:(0,i,0))],
        out_specs=pl.BlockSpec((OB,128,128),lambda i:(i,0,0)),
        scratch_shapes=[pltpu.VMEM((128*OB,128),f32)],
        compiler_params=pltpu.CompilerParams(vmem_limit_bytes=40<<20),
        name="relayout")(ops_t)


def m2l_body(T,U,OG,src_ref,dst_ref,cls_ref,want_ref,blk_ref,own_ref,ag_ref,ops_ref,out_ref,tab,tmp,dense):
    tab[0:BOX,:]=own_ref[...].astype(f32)
    tab[ZROW:ZROW+8,:]=jnp.zeros((8,128),f32)
    def reach(n,_):
        r0=pl.multiple_of(blk_ref[n]*BOX,BOX)
        tmp[...]=ag_ref[pl.ds(r0,BOX),:].astype(f32)
        d0=pl.multiple_of(BOX+n*CAP,8)
        for u in range(CAP):
            w=want_ref.at[pl.ds(u,(NEAR-1)*CAP+1)][n*CAP]
            tab[pl.ds(d0+u,1),:]=tmp[pl.ds(w,1),:]
        return 0
    lax.fori_loop(0,NEAR,reach,0)
    for h in range(BOX//T):
        def zero(i,_):
            dense[pl.ds(pl.multiple_of(i*512,512),512),:]=jnp.zeros((512,128),f32)
            return 0
        lax.fori_loop(0,OP*T//512,zero,0)
        def box(i,_):
            t=h*T+i
            def chunk(c,_):
                b=c*(U*BOX)+t
                for u in range(U):
                    w=pl.ds(u*BOX,(KP-U)*BOX+BOX)
                    dense[pl.ds(dst_ref.at[w][b],1),:]=tab[pl.ds(src_ref.at[w][b],1),:]
                return 0
            lax.fori_loop(0,cls_ref[t],chunk,0)
            return 0
        lax.fori_loop(0,T,box,0)
        def mm(k,acc):
            ls=[dense[pl.ds(pl.multiple_of((k*OG+j)*T,T),T),:].astype(bf16) for j in range(OG)]
            r=ops_ref[pl.ds(pl.multiple_of(k*OG*128,128),OG*128),:]
            return acc+jnp.dot(jnp.concatenate(ls,1),r,preferred_element_type=f32)
        acc=lax.fori_loop(0,OP//OG,mm,jnp.zeros((T,128),f32))
        out_ref[h*T:(h+1)*T,:]=acc[:,:COEF]

def m2l(src,dst,cls,want,blk,own,ag,ops,T=128,U=16,OG=20):
    sm=pl.BlockSpec(memory_space=pltpu.SMEM); vm=pl.BlockSpec(memory_space=pltpu.VMEM)
    return pl.pallas_call(functools.partial(m2l_body,T,U,OG),
        out_shape=jax.ShapeDtypeStruct((BOX,COEF),f32),
        in_specs=[sm]*5+[vm]*3, out_specs=vm,
        scratch_shapes=[pltpu.VMEM((NTAB,128),f32),pltpu.VMEM((BOX,128),f32),pltpu.VMEM((OP*T+8,128),f32)],
        compiler_params=pltpu.CompilerParams(vmem_limit_bytes=56<<20),
        name="m2l")(src,dst,cls,want,blk,own,ag,ops)

def slots(m2l_source,m2l_offset,cnt,T=128,U=16):
    k=lax.broadcasted_iota(jnp.int32,(KMAX,BOX),0)
    t=lax.broadcasted_iota(jnp.int32,(KMAX,BOX),1)
    s=jnp.where(k<cnt[None,:],m2l_source.T,ZROW)
    d=m2l_offset.T*T+(t&(T-1))
    s=jnp.pad(s,((0,KP-KMAX),(0,0)),constant_values=ZROW).reshape(-1)
    d=jnp.pad(d,((0,KP-KMAX),(0,0)),constant_values=OP*T).reshape(-1)
    return s,d,lax.div(cnt+U-1,U)

def ring(x,by,n):
    return lax.ppermute(x,AXES,[(i,i+by) for i in range(n) if 0<=i+by<n])

def shards(gx,gy,multipoles,m2l_ops,want_boxes,m2l_source,m2l_offset,m2l_count,positions,charges,part_count,
           pair_target,pair_source,pair_offset,pair_count):
    n=gx*gy
    x,y=lax.axis_index("gx"),lax.axis_index("gy")
    live=lax.broadcasted_iota(jnp.int32,(BOX,PB),1)<part_count[:,None]
    own4=jnp.concatenate([positions.transpose(1,0,2),jnp.where(live,charges,0.0)[None]],0)
    nxt4=ring(own4,-1,n)
    own=jnp.pad(multipoles,((0,0),(0,128-COEF)))
    half=gy//2
    swap=[]
    for g in range(gx):
        for j in range(gy):
            to=g+1 if j>=half else g-1
            if 0<=to<gx: swap.append((g*gy+j,to*gy+j))
    other=lax.ppermute(own,AXES,swap)
    ag=lax.all_gather(jnp.stack([own,other]),"gy").reshape(-1,128)
    me=x*gy+y
    reach=jnp.arange(NEAR,dtype=jnp.int32)
    peer=jnp.clip(me+reach-NEAR//2+(reach>=NEAR//2).astype(jnp.int32),0,n-1)
    px,py=lax.div(peer,gy),lax.rem(peer,gy)
    blk=py*2+(px!=x).astype(jnp.int32)
    ops=relayout(m2l_ops.transpose(1,0,2)).reshape(-1,128)
    field,fwd=near(pair_target[0],pair_source[0],pair_offset[0],pair_count,own4,nxt4)
    back=ring(fwd,1,n)
    s,d,c=slots(m2l_source,m2l_offset,m2l_count)
    local_exp=m2l(s,d,c,want_boxes.reshape(-1),blk,own,ag,ops)
    return local_exp,jnp.where(live,field+back,0.0)

def solution(mesh):
    both=AXES
    placed=(P(both,None),P(),P(both,None,None),P(both,None),P(both,None),P(both),P(both,None,None),P(both,None),P(both),
            P(both,None),P(both,None),P(both,None),P(both))
    return jax.shard_map(functools.partial(shards,mesh.shape["gx"],mesh.shape["gy"]),mesh=mesh,in_specs=placed,
        out_specs=(P(both,None),P(both,None)),check_vma=False)
```

```python
import functools

import jax
import jax.numpy as jnp
from jax import lax
from jax.experimental import pallas as pl
from jax.experimental.pallas import tpu as pltpu
from jax.sharding import PartitionSpec as P

BOX, PB, EPS = 256, 128, 0.0025
OFFS, OP, KMAX, KP, COEF, NEAR, CAP = 316, 320, 189, 208, 121, 16, 128
ZROW = BOX + NEAR * CAP
NTAB = ZROW + 8
DROW = OFFS * BOX
LST = 3200
f32, bf16 = jnp.float32, jnp.bfloat16
AXES = ("gx", "gy")

def split3(v):
    a=v.astype(bf16).astype(f32); r=v-a
    b=r.astype(bf16).astype(f32); c=r-b
    return a,b,c

def near_body(U,PU,tgt_ref,src_ref,off_ref,cnt_ref,own_ref,nxt_ref,tcol_ref,srow_ref,out_ref,fwd_ref,xb,fa,qa,cc,dd,vv):
    sub=lax.broadcasted_iota(jnp.int32,(8,128),0)
    m3=(sub<3).astype(f32)
    one=jnp.ones((8,128),f32); zero=jnp.zeros((8,128),f32)
    for o in range(27):
        v=(o//9-1,(o//3)%3-1,o%3-1)
        vv[o]=jnp.where(sub==0,float(v[0]),jnp.where(sub==1,float(v[1]),jnp.where(sub==2,float(v[2]),0.0)))
    def rows(g,_):
        for half,ref in ((0,own_ref),(1,nxt_ref)):
            for c in range(4):
                p=ref[c,pl.ds(pl.multiple_of(g*8,8),8),:]
                if c<3: p=p-0.5
                xb[pl.ds(half*BOX*8+g*64+c,8,stride=8),:]=p
            for c in range(4,8):
                xb[pl.ds(half*BOX*8+g*64+c,8,stride=8),:]=zero
        return 0
    lax.fori_loop(0,BOX//8,rows,0)
    def feat_b(y):
        y1,y2,y3=split3(y)
        q1,q2,q3=split3(y*y)
        return jnp.concatenate([y1,y1,y1,y2,y2,y3,q1,q2,q3,one]+[zero]*6,0).astype(bf16)
    diag=lax.broadcasted_iota(jnp.int32,(PB,PB),0)==lax.broadcasted_iota(jnp.int32,(PB,PB),1)
    def sq(b):
        return xb[pl.ds(pl.multiple_of(b*8,8),8),:]
    def prep(g,_):
        for u in range(PU):
            b=g*PU+u
            x=sq(b)
            x1,x2,x3=split3(x*-2.0)
            xm=x*m3
            s=jnp.sum(xm*xm,axis=0,keepdims=True)+EPS
            s=jnp.broadcast_to(s,(8,128))
            s1,s2,s3=split3(s)
            sr=jnp.where(sub==0,s1,jnp.where(sub==1,s2,jnp.where(sub==2,s3,0.0)))
            x1,x2,x3=x1*m3,x2*m3,x3*m3
            f=jnp.concatenate([x1,x2,x3,x1,x2,x1,m3,m3,m3,sr,x]+[zero]*5,0)
            t=f.T
            ft=jnp.where(lax.broadcasted_iota(jnp.int32,(PB,128),1)<80,t,0.0).astype(bf16)
            fa[b]=ft
            q=jnp.broadcast_to(t[:,83:84],(PB,PB))
            qa[b]=q
            k=lax.rsqrt(jnp.dot(ft,feat_b(x),preferred_element_type=f32))
            k=jnp.where(diag,0.0,k)
            out_ref[pl.ds(b,1),:]=jnp.sum(k*q,axis=0,keepdims=True)
        return 0
    lax.fori_loop(0,BOX//PU,prep,0)
    n=cnt_ref[0]
    def zinit(i,_):
        dd[pl.ds(pl.multiple_of(i*8,8),8),:]=zero
        cc[pl.ds(pl.multiple_of(i*8,8),8),:]=zero
        return 0
    lax.fori_loop(0,128,zinit,0)
    lane=lax.broadcasted_iota(jnp.int32,(PB,128),1)
    if True:
        def pairs(g,_):
            cs=[]
            for u in range(U):
                p=g*U+u
                a=tgt_ref[p]; b=src_ref[p]; o=off_ref[p]
                y=sq(b)+vv[o]
                k=lax.rsqrt(jnp.dot(fa[a],feat_b(y),preferred_element_type=f32))
                qb=xb[pl.ds(b*8+3,1),:]
                dd[pl.ds(p,1),:]=jnp.sum(k*qa[a],axis=0,keepdims=True)
                cs.append(jnp.sum(k*qb,axis=1,keepdims=True))
            blk=lax.shift_right_logical(g*U,7)
            l0=(g*U)&127
            r=pl.ds(pl.multiple_of(blk*128,128),128)
            c=cc[r,:]
            for u in range(U):
                c=jnp.where(lane==l0+u,cs[u],c)
            cc[r,:]=c
            return 0
        lax.fori_loop(0,lax.div(n+U-1,U),pairs,0)
    fwd_ref[...]=jnp.zeros_like(fwd_ref)
    def scat(k,_):
        r=pl.ds(pl.multiple_of(k*128,128),128)
        prow=k*128+lax.broadcasted_iota(jnp.int32,(1,128),1)
        tid=jnp.where(prow<n,tcol_ref[pl.ds(k,1),:],-1)
        sid=jnp.where(prow<n,srow_ref[pl.ds(k,1),:],-1)
        oh_t=(lax.broadcasted_iota(jnp.int32,(BOX,128),0)==tid).astype(f32).astype(bf16)
        oh_s=(lax.broadcasted_iota(jnp.int32,(2*BOX,128),0)==sid).astype(f32).astype(bf16)
        c1,c2,c3=split3(cc[r,:])
        d1,d2,d3=split3(dd[r,:])
        nt=(((1,),(1,)),((),()))
        ct=sum(lax.dot_general(oh_t,c.astype(bf16),nt,preferred_element_type=f32) for c in (c1,c2,c3))
        ds=sum(jnp.dot(oh_s,d.astype(bf16),preferred_element_type=f32) for d in (d1,d2,d3))
        out_ref[...]+=ct+ds[:BOX]
        fwd_ref[...]+=ds[BOX:]
        return 0
    lax.fori_loop(0,lax.div(n+127,128),scat,0)

def near(tgt,src,off,cnt,own4,nxt4,U=32,PU=16):
    sm=pl.BlockSpec(memory_space=pltpu.SMEM); vm=pl.BlockSpec(memory_space=pltpu.VMEM)
    return pl.pallas_call(functools.partial(near_body,U,PU),
        out_shape=(jax.ShapeDtypeStruct((BOX,PB),f32),jax.ShapeDtypeStruct((BOX,PB),f32)),
        in_specs=[sm]*4+[vm]*4,
        out_specs=(vm,vm),
        scratch_shapes=[pltpu.VMEM((2*BOX*8,128),f32),pltpu.VMEM((BOX,PB,128),bf16),pltpu.VMEM((BOX,PB,128),f32),
            pltpu.VMEM((1024,128),f32),pltpu.VMEM((1024,128),f32),pltpu.VMEM((27,8,128),f32)],
        compiler_params=pltpu.CompilerParams(vmem_limit_bytes=56<<20),
        name="near")(tgt,src,off,cnt,own4,nxt4,tgt.reshape(8,128),src.reshape(8,128))

def swap8(rows,masks):
    rows=list(rows)
    for s,m in zip((4,2,1),masks):
        for i in range(8):
            if i&s: continue
            a,b=rows[i],rows[i+s]
            rows[i]=jnp.where(m,a,pltpu.roll(b,s,0))
            rows[i+s]=jnp.where(m,pltpu.roll(a,8-s,0),b)
    return rows

def relayout_body(in_ref,out_ref,buf):
    OB=in_ref.shape[1]
    @pl.when(pl.program_id(0)==0)
    def _():
        buf[...]=jnp.zeros_like(buf)
    for c in range(COEF):
        buf[c*OB:(c+1)*OB,:COEF]=in_ref[c].astype(f32)
    sub=lax.broadcasted_iota(jnp.int32,(8,128),0)
    masks=[(sub&s)==0 for s in (4,2,1)]
    for o in range(0,OB,8):
        for c in range(0,128,16):
            lo=swap8([buf[(c+i)*OB+o:(c+i)*OB+o+8,:] for i in range(8)],masks)
            hi=swap8([buf[(c+8+i)*OB+o:(c+8+i)*OB+o+8,:] for i in range(8)],masks)
            for i in range(8):
                out_ref[o+i,c:c+16,:]=jnp.concatenate([lo[i],hi[i]],0).astype(bf16)

def relayout(ops_t,OB=32):
    return pl.pallas_call(relayout_body,
        out_shape=jax.ShapeDtypeStruct((OP,128,128),bf16),
        grid=(OP//OB,),
        in_specs=[pl.BlockSpec((COEF,OB,COEF),lambda i:(0,i,0))],
        out_specs=pl.BlockSpec((OB,128,128),lambda i:(i,0,0)),
        scratch_shapes=[pltpu.VMEM((128*OB,128),f32)],
        compiler_params=pltpu.CompilerParams(vmem_limit_bytes=40<<20),
        name="relayout")(ops_t)

def m2l_body(U,B,OG,num_ref,want_ref,blk_ref,src_hbm,dst_hbm,lst_hbm,own_hbm,ag_hbm,ops_hbm,out_ref,
             src_ref,dst_ref,lst_ref,own_ref,ag_ref,ops,tab,tmp,dense,sem):
    T=BOX
    cps=[pltpu.make_async_copy(a,b,sem.at[i]) for i,(a,b) in enumerate(
        ((own_hbm,own_ref),(ag_hbm,ag_ref),(src_hbm,src_ref),(dst_hbm,dst_ref),(lst_hbm,lst_ref),(ops_hbm,ops)))]
    for c in cps: c.start()
    def zero(i,_):
        dense[pl.ds(pl.multiple_of(i*512,512),512),:]=jnp.zeros((512,128),f32)
        return 0
    lax.fori_loop(0,OFFS*T//512,zero,0)
    cps[0].wait()
    cps[1].wait()
    tab[0:BOX,:]=own_ref[...].astype(f32)
    tab[ZROW:ZROW+8,:]=jnp.zeros((8,128),f32)
    def reach(n,_):
        r0=pl.multiple_of(blk_ref[n]*BOX,BOX)
        tmp[...]=ag_ref[pl.ds(r0,BOX),:].astype(f32)
        d0=pl.multiple_of(BOX+n*CAP,8)
        for u in range(CAP):
            w=want_ref.at[pl.ds(u,(NEAR-1)*CAP+1)][n*CAP]
            tab[pl.ds(d0+u,1),:]=tmp[pl.ds(w,1),:]
        return 0
    lax.fori_loop(0,NEAR,reach,0)
    for c in cps[2:5]: c.wait()
    def chunk(i,_):
        for v in range(B):
            b=lst_ref.at[pl.ds(v,3072)][i*B]
            for u in range(U):
                w=pl.ds(u*BOX,(KP-U)*BOX+BOX)
                dense[pl.ds(dst_ref.at[w][b],1),:]=tab[pl.ds(src_ref.at[w][b],1),:]
        return 0
    lax.fori_loop(0,num_ref[0],chunk,0)
    cps[5].wait()
    out_ref[...]=jnp.zeros_like(out_ref)
    def part(o,n):
        ls=[dense[pl.ds(pl.multiple_of((o+j)*T,T),T),:].astype(bf16) for j in range(n)]
        r=ops[pl.ds(pl.multiple_of(o*128,128),n*128),:]
        out_ref[...]+=jnp.dot(jnp.concatenate(ls,1),r,preferred_element_type=f32)[:,:COEF]
    NS=OFFS//OG
    def mm(k,_):
        part(k*OG,OG)
        return 0
    lax.fori_loop(0,NS,mm,0)
    if OFFS%OG: part(NS*OG,OFFS%OG)

def m2l(src,dst,lst,num,want,blk,own,ag,ops,U=16,B=8,OG=20):
    sm=pl.BlockSpec(memory_space=pltpu.SMEM); vm=pl.BlockSpec(memory_space=pltpu.VMEM); hb=pl.BlockSpec(memory_space=pl.ANY)
    return pl.pallas_call(functools.partial(m2l_body,U,B,OG),
        out_shape=jax.ShapeDtypeStruct((BOX,COEF),f32),
        in_specs=[sm]*3+[hb]*6, out_specs=vm,
        scratch_shapes=[pltpu.SMEM((KP*BOX,),jnp.int32),pltpu.SMEM((KP*BOX,),jnp.int32),pltpu.SMEM((LST,),jnp.int32),
            pltpu.VMEM((BOX,128),bf16),pltpu.VMEM(ag.shape,bf16),pltpu.VMEM((OP*128,128),bf16),
            pltpu.VMEM((NTAB,128),f32),pltpu.VMEM((BOX,128),f32),pltpu.VMEM((DROW+8,128),f32),pltpu.SemaphoreType.DMA((6,))],
        compiler_params=pltpu.CompilerParams(vmem_limit_bytes=58<<20),
        name="m2l")(num,want,blk,src,dst,lst,own,ag,ops)

def slots(srcT,offT,cnt,U=16,B=8):
    k=lax.broadcasted_iota(jnp.int32,(KMAX,BOX),0)
    t=lax.broadcasted_iota(jnp.int32,(KMAX,BOX),1)
    s=jnp.where(k<cnt[None,:],srcT,ZROW)
    d=offT*BOX+t
    s=jnp.pad(s,((0,KP-KMAX),(0,0)),constant_values=ZROW).reshape(-1)
    d=jnp.pad(d,((0,KP-KMAX),(0,0)),constant_values=DROW).reshape(-1)
    n=lax.div(cnt+U-1,U)
    a=jnp.arange(BOX,dtype=jnp.int32)
    incl=jnp.sum(jnp.where(a[None,:]<=a[:,None],n[None,:],0),1)
    i=jnp.arange(LST,dtype=jnp.int32)
    m=incl[None,:]<=i[:,None]
    bx=jnp.sum(m.astype(jnp.int32),1)
    ex=jnp.sum(jnp.where(m,n[None,:],0),1)
    lst=jnp.where(bx<BOX,bx+(i-ex)*(U*BOX),192*BOX)
    num=lax.div(jnp.sum(n)+B-1,B)
    return s,d,lst,num[None]

def ring(x,by,n):
    return lax.ppermute(x,AXES,[(i,i+by) for i in range(n) if 0<=i+by<n])

def shards(gx,gy,multipoles,m2l_ops,want_boxes,m2l_source,m2l_offset,m2l_count,positions,charges,part_count,
           pair_target,pair_source,pair_offset,pair_count):
    n=gx*gy
    x,y=lax.axis_index("gx"),lax.axis_index("gy")
    live=lax.broadcasted_iota(jnp.int32,(BOX,PB),1)<part_count[:,None]
    own4=jnp.concatenate([positions.transpose(1,0,2),jnp.where(live,charges,0.0)[None]],0)
    nxt4=ring(own4,-1,n)
    own=jnp.pad(multipoles,((0,0),(0,128-COEF)))
    half=gy//2
    swap=[]
    for g in range(gx):
        for j in range(gy):
            to=g+1 if j>=half else g-1
            if 0<=to<gx: swap.append((g*gy+j,to*gy+j))
    other=lax.ppermute(own,AXES,swap)
    ag=lax.all_gather(jnp.stack([own,other]),"gy").reshape(-1,128)
    me=x*gy+y
    reach=jnp.arange(NEAR,dtype=jnp.int32)
    peer=jnp.clip(me+reach-NEAR//2+(reach>=NEAR//2).astype(jnp.int32),0,n-1)
    px,py=lax.div(peer,gy),lax.rem(peer,gy)
    blk=py*2+(px!=x).astype(jnp.int32)
    s,d,lst,num=slots(m2l_source.T,m2l_offset.T,m2l_count)
    ops=relayout(m2l_ops.transpose(1,0,2)).reshape(-1,128)
    nxt4,ops,s,d,lst,num,blk=lax.optimization_barrier((nxt4,ops,s,d,lst,num,blk))
    field,fwd=near(pair_target[0],pair_source[0],pair_offset[0],pair_count,own4,nxt4)
    back=ring(fwd,1,n)
    local_exp=m2l(s,d,lst,num,want_boxes.reshape(-1),blk,own,ag,ops)
    return local_exp,jnp.where(live,field+back,0.0)

def solution(mesh):
    both=AXES
    placed=(P(both,None),P(),P(both,None,None),P(both,None),P(both,None),P(both),P(both,None,None),P(both,None),P(both),
            P(both,None),P(both,None),P(both,None),P(both))
    return jax.shard_map(functools.partial(shards,mesh.shape["gx"],mesh.shape["gy"]),mesh=mesh,in_specs=placed,
        out_specs=(P(both,None),P(both,None)),check_vma=False)
```

```python
import functools

import jax
import jax.numpy as jnp
from jax import lax
from jax.experimental import pallas as pl
from jax.experimental.pallas import tpu as pltpu
from jax.sharding import PartitionSpec as P

BOX, PB, EPS = 256, 128, 0.0025
OFFS, OP, KMAX, KP, COEF, NEAR, CAP = 316, 320, 189, 208, 121, 16, 128
ZROW = BOX + NEAR * CAP
NTAB = ZROW + 8
DROW = OFFS * BOX
LST = 3200
f32, bf16 = jnp.float32, jnp.bfloat16
AXES = ("gx", "gy")

def split3(v):
    a=v.astype(bf16).astype(f32); r=v-a
    b=r.astype(bf16).astype(f32); c=r-b
    return a,b,c

def near_body(U,PU,tgt_ref,src_ref,off_ref,cnt_ref,own_ref,nxt_ref,tcol_ref,srow_ref,out_ref,fwd_ref,xb,fa,qa,cc,dd,vv):
    sub=lax.broadcasted_iota(jnp.int32,(8,128),0)
    m3=(sub<3).astype(f32)
    one=jnp.ones((8,128),f32); zero=jnp.zeros((8,128),f32)
    for o in range(27):
        v=(o//9-1,(o//3)%3-1,o%3-1)
        vv[o]=jnp.where(sub==0,float(v[0]),jnp.where(sub==1,float(v[1]),jnp.where(sub==2,float(v[2]),0.0)))
    def rows(g,_):
        for half,ref in ((0,own_ref),(1,nxt_ref)):
            for c in range(4):
                p=ref[c,pl.ds(pl.multiple_of(g*8,8),8),:]
                if c<3: p=p-0.5
                xb[pl.ds(half*BOX*8+g*64+c,8,stride=8),:]=p
            for c in range(4,8):
                xb[pl.ds(half*BOX*8+g*64+c,8,stride=8),:]=zero
        return 0
    lax.fori_loop(0,BOX//8,rows,0)
    def feat_b(y):
        y1,y2,y3=split3(y)
        q1,q2,q3=split3(y*y)
        return jnp.concatenate([y1,y1,y1,y2,y2,y3,q1,q2,q3,one]+[zero]*6,0).astype(bf16)
    diag=lax.broadcasted_iota(jnp.int32,(PB,PB),0)==lax.broadcasted_iota(jnp.int32,(PB,PB),1)
    def sq(b):
        return xb[pl.ds(pl.multiple_of(b*8,8),8),:]
    def prep(g,_):
        for u in range(PU):
            b=g*PU+u
            x=sq(b)
            x1,x2,x3=split3(x*-2.0)
            xm=x*m3
            s=jnp.sum(xm*xm,axis=0,keepdims=True)+EPS
            s=jnp.broadcast_to(s,(8,128))
            s1,s2,s3=split3(s)
            sr=jnp.where(sub==0,s1,jnp.where(sub==1,s2,jnp.where(sub==2,s3,0.0)))
            x1,x2,x3=x1*m3,x2*m3,x3*m3
            f=jnp.concatenate([x1,x2,x3,x1,x2,x1,m3,m3,m3,sr,x]+[zero]*5,0)
            t=f.T
            ft=jnp.where(lax.broadcasted_iota(jnp.int32,(PB,128),1)<80,t,0.0).astype(bf16)
            fa[b]=ft
            q=jnp.broadcast_to(t[:,83:84],(PB,PB))
            qa[b]=q
            k=lax.rsqrt(jnp.dot(ft,feat_b(x),preferred_element_type=f32))
            k=jnp.where(diag,0.0,k)
            out_ref[pl.ds(b,1),:]=jnp.sum(k*q,axis=0,keepdims=True)
        return 0
    lax.fori_loop(0,BOX//PU,prep,0)
    n=cnt_ref[0]
    def zinit(i,_):
        dd[pl.ds(pl.multiple_of(i*8,8),8),:]=zero
        cc[pl.ds(pl.multiple_of(i*8,8),8),:]=zero
        return 0
    lax.fori_loop(0,128,zinit,0)
    lane=lax.broadcasted_iota(jnp.int32,(PB,128),1)
    if True:
        def pairs(g,_):
            blk=lax.shift_right_logical(g*U,7)
            l0=(g*U)&127
            r=pl.ds(pl.multiple_of(blk*128,128),128)
            c=cc[r,:]
            for u in range(U):
                p=g*U+u
                a=tgt_ref[p]; b=src_ref[p]; o=off_ref[p]
                y=sq(b)+vv[o]
                k=lax.rsqrt(jnp.dot(fa[a],feat_b(y),preferred_element_type=f32))
                qb=xb[pl.ds(b*8+3,1),:]
                dd[pl.ds(p,1),:]=jnp.sum(k*qa[a],axis=0,keepdims=True)
                c=jnp.where(lane==l0+u,jnp.sum(k*qb,axis=1,keepdims=True),c)
            cc[r,:]=c
            return 0
        lax.fori_loop(0,lax.div(n+U-1,U),pairs,0)
    fwd_ref[...]=jnp.zeros_like(fwd_ref)
    def scat(k,_):
        r=pl.ds(pl.multiple_of(k*128,128),128)
        prow=k*128+lax.broadcasted_iota(jnp.int32,(1,128),1)
        tid=jnp.where(prow<n,tcol_ref[pl.ds(k,1),:],-1)
        sid=jnp.where(prow<n,srow_ref[pl.ds(k,1),:],-1)
        oh_t=(lax.broadcasted_iota(jnp.int32,(BOX,128),0)==tid).astype(f32).astype(bf16)
        oh_s=(lax.broadcasted_iota(jnp.int32,(2*BOX,128),0)==sid).astype(f32).astype(bf16)
        c1,c2,c3=split3(cc[r,:])
        d1,d2,d3=split3(dd[r,:])
        nt=(((1,),(1,)),((),()))
        ct=sum(lax.dot_general(oh_t,c.astype(bf16),nt,preferred_element_type=f32) for c in (c1,c2,c3))
        ds=sum(jnp.dot(oh_s,d.astype(bf16),preferred_element_type=f32) for d in (d1,d2,d3))
        out_ref[...]+=ct+ds[:BOX]
        fwd_ref[...]+=ds[BOX:]
        return 0
    lax.fori_loop(0,lax.div(n+127,128),scat,0)

def near(tgt,src,off,cnt,own4,nxt4,U=64,PU=32):
    sm=pl.BlockSpec(memory_space=pltpu.SMEM); vm=pl.BlockSpec(memory_space=pltpu.VMEM)
    return pl.pallas_call(functools.partial(near_body,U,PU),
        out_shape=(jax.ShapeDtypeStruct((BOX,PB),f32),jax.ShapeDtypeStruct((BOX,PB),f32)),
        in_specs=[sm]*4+[vm]*4,
        out_specs=(vm,vm),
        scratch_shapes=[pltpu.VMEM((2*BOX*8,128),f32),pltpu.VMEM((BOX,PB,128),bf16),pltpu.VMEM((BOX,PB,128),f32),
            pltpu.VMEM((1024,128),f32),pltpu.VMEM((1024,128),f32),pltpu.VMEM((27,8,128),f32)],
        compiler_params=pltpu.CompilerParams(vmem_limit_bytes=56<<20),
        name="near")(tgt,src,off,cnt,own4,nxt4,tgt.reshape(8,128),src.reshape(8,128))

def swap8(rows,masks):
    rows=list(rows)
    for s,m in zip((4,2,1),masks):
        for i in range(8):
            if i&s: continue
            a,b=rows[i],rows[i+s]
            rows[i]=jnp.where(m,a,pltpu.roll(b,s,0))
            rows[i+s]=jnp.where(m,pltpu.roll(a,8-s,0),b)
    return rows

def relayout_body(in_ref,out_ref,buf):
    OB=in_ref.shape[1]
    for c in range(COEF):
        buf[c*OB:(c+1)*OB,:COEF]=in_ref[c].astype(f32)
    sub=lax.broadcasted_iota(jnp.int32,(8,128),0)
    masks=[(sub&s)==0 for s in (4,2,1)]
    for o in range(0,OB,8):
        for c in range(0,128,16):
            lo=swap8([buf[(c+i)*OB+o:(c+i)*OB+o+8,:] for i in range(8)],masks)
            hi=swap8([buf[(c+8+i)*OB+o:(c+8+i)*OB+o+8,:] for i in range(8)],masks)
            for i in range(8):
                out_ref[o+i,c:c+16,:]=jnp.concatenate([lo[i],hi[i]],0).astype(bf16)

def relayout(ops_t,OB=32):
    def outer(src,dst,buf):
        buf[...]=jnp.zeros_like(buf)
        pltpu.emit_pipeline(lambda i,o: relayout_body(i,o,buf),grid=(OP//OB,),
            in_specs=[pl.BlockSpec((COEF,OB,COEF),lambda i:(0,i,0))],
            out_specs=[pl.BlockSpec((OB,128,128),lambda i:(i,0,0))])(src,dst)
    hb=pl.BlockSpec(memory_space=pltpu.HBM)
    return pl.pallas_call(outer,
        out_shape=jax.ShapeDtypeStruct((OP,128,128),bf16),
        in_specs=[hb],out_specs=hb,
        scratch_shapes=[pltpu.VMEM((128*OB,128),f32)],
        compiler_params=pltpu.CompilerParams(vmem_limit_bytes=60<<20),
        name="relayout")(ops_t)

def m2l_body(U,B,OG,num_ref,want_ref,blk_ref,src_hbm,dst_hbm,lst_hbm,own_hbm,ag_hbm,ops_hbm,out_ref,
             src_ref,dst_ref,lst_ref,own_ref,ag_ref,ops,tab,tmp,dense,sem):
    T=BOX
    cps=[pltpu.make_async_copy(a,b,sem.at[i]) for i,(a,b) in enumerate(
        ((own_hbm,own_ref),(ag_hbm,ag_ref),(src_hbm,src_ref),(dst_hbm,dst_ref),(lst_hbm,lst_ref),(ops_hbm,ops)))]
    for c in cps: c.start()
    def zero(i,_):
        dense[pl.ds(pl.multiple_of(i*512,512),512),:]=jnp.zeros((512,128),f32)
        return 0
    lax.fori_loop(0,OFFS*T//512,zero,0)
    cps[0].wait()
    cps[1].wait()
    tab[0:BOX,:]=own_ref[...].astype(f32)
    tab[ZROW:ZROW+8,:]=jnp.zeros((8,128),f32)
    def reach(n,_):
        r0=pl.multiple_of(blk_ref[n]*BOX,BOX)
        tmp[...]=ag_ref[pl.ds(r0,BOX),:].astype(f32)
        d0=pl.multiple_of(BOX+n*CAP,8)
        for u in range(CAP):
            w=want_ref.at[pl.ds(u,(NEAR-1)*CAP+1)][n*CAP]
            tab[pl.ds(d0+u,1),:]=tmp[pl.ds(w,1),:]
        return 0
    lax.fori_loop(0,NEAR,reach,0)
    for c in cps[2:5]: c.wait()
    def chunk(i,_):
        for v in range(B):
            b=lst_ref.at[pl.ds(v,3072)][i*B]
            for u in range(U):
                w=pl.ds(u*BOX,(KP-U)*BOX+BOX)
                dense[pl.ds(dst_ref.at[w][b],1),:]=tab[pl.ds(src_ref.at[w][b],1),:]
        return 0
    lax.fori_loop(0,num_ref[0],chunk,0)
    cps[5].wait()
    out_ref[...]=jnp.zeros_like(out_ref)
    def part(o,n):
        ls=[dense[pl.ds(pl.multiple_of((o+j)*T,T),T),:].astype(bf16) for j in range(n)]
        r=ops[pl.ds(pl.multiple_of(o*128,128),n*128),:]
        out_ref[...]+=jnp.dot(jnp.concatenate(ls,1),r,preferred_element_type=f32)[:,:COEF]
    NS=OFFS//OG
    def mm(k,_):
        part(k*OG,OG)
        return 0
    lax.fori_loop(0,NS,mm,0)
    if OFFS%OG: part(NS*OG,OFFS%OG)

def m2l(src,dst,lst,num,want,blk,own,ag,ops,U=16,B=8,OG=20):
    sm=pl.BlockSpec(memory_space=pltpu.SMEM); vm=pl.BlockSpec(memory_space=pltpu.VMEM); hb=pl.BlockSpec(memory_space=pl.ANY)
    return pl.pallas_call(functools.partial(m2l_body,U,B,OG),
        out_shape=jax.ShapeDtypeStruct((BOX,COEF),f32),
        in_specs=[sm]*3+[hb]*6, out_specs=vm,
        scratch_shapes=[pltpu.SMEM((KP*BOX,),jnp.int32),pltpu.SMEM((KP*BOX,),jnp.int32),pltpu.SMEM((LST,),jnp.int32),
            pltpu.VMEM((BOX,128),bf16),pltpu.VMEM(ag.shape,bf16),pltpu.VMEM((OP*128,128),bf16),
            pltpu.VMEM((NTAB,128),f32),pltpu.VMEM((BOX,128),f32),pltpu.VMEM((DROW+8,128),f32),pltpu.SemaphoreType.DMA((6,))],
        compiler_params=pltpu.CompilerParams(vmem_limit_bytes=58<<20),
        name="m2l")(num,want,blk,src,dst,lst,own,ag,ops)

def slots(srcT,offT,cnt,U=16,B=8):
    k=lax.broadcasted_iota(jnp.int32,(KMAX,BOX),0)
    t=lax.broadcasted_iota(jnp.int32,(KMAX,BOX),1)
    s=jnp.where(k<cnt[None,:],srcT,ZROW)
    d=offT*BOX+t
    s=jnp.pad(s,((0,KP-KMAX),(0,0)),constant_values=ZROW).reshape(-1)
    d=jnp.pad(d,((0,KP-KMAX),(0,0)),constant_values=DROW).reshape(-1)
    n=lax.div(cnt+U-1,U)
    a=jnp.arange(BOX,dtype=jnp.int32)
    incl=jnp.sum(jnp.where(a[None,:]<=a[:,None],n[None,:],0),1)
    i=jnp.arange(LST,dtype=jnp.int32)
    m=incl[None,:]<=i[:,None]
    bx=jnp.sum(m.astype(jnp.int32),1)
    ex=jnp.sum(jnp.where(m,n[None,:],0),1)
    lst=jnp.where(bx<BOX,bx+(i-ex)*(U*BOX),192*BOX)
    num=lax.div(jnp.sum(n)+B-1,B)
    return s,d,lst,num[None]

def ring(x,by,n):
    return lax.ppermute(x,AXES,[(i,i+by) for i in range(n) if 0<=i+by<n])

def shards(gx,gy,multipoles,m2l_ops,want_boxes,m2l_source,m2l_offset,m2l_count,positions,charges,part_count,
           pair_target,pair_source,pair_offset,pair_count):
    n=gx*gy
    x,y=lax.axis_index("gx"),lax.axis_index("gy")
    live=lax.broadcasted_iota(jnp.int32,(BOX,PB),1)<part_count[:,None]
    own4=jnp.concatenate([positions.transpose(1,0,2),jnp.where(live,charges,0.0)[None]],0)
    nxt4=ring(own4,-1,n)
    own=jnp.pad(multipoles,((0,0),(0,128-COEF)))
    half=gy//2
    swap=[]
    for g in range(gx):
        for j in range(gy):
            to=g+1 if j>=half else g-1
            if 0<=to<gx: swap.append((g*gy+j,to*gy+j))
    other=lax.ppermute(own,AXES,swap)
    ag=lax.all_gather(jnp.stack([own,other]),"gy").reshape(-1,128)
    me=x*gy+y
    reach=jnp.arange(NEAR,dtype=jnp.int32)
    peer=jnp.clip(me+reach-NEAR//2+(reach>=NEAR//2).astype(jnp.int32),0,n-1)
    px,py=lax.div(peer,gy),lax.rem(peer,gy)
    blk=py*2+(px!=x).astype(jnp.int32)
    s,d,lst,num=slots(m2l_source.T,m2l_offset.T,m2l_count)
    ops=relayout(m2l_ops.transpose(1,0,2)).reshape(-1,128)
    nxt4,ops,s,d,lst,num,blk=lax.optimization_barrier((nxt4,ops,s,d,lst,num,blk))
    field,fwd=near(pair_target[0],pair_source[0],pair_offset[0],pair_count,own4,nxt4)
    back=ring(fwd,1,n)
    local_exp=m2l(s,d,lst,num,want_boxes.reshape(-1),blk,own,ag,ops)
    local_exp,back,field=lax.optimization_barrier((local_exp,back,field))
    return local_exp,jnp.where(live,field+back,0.0)

def solution(mesh):
    both=AXES
    placed=(P(both,None),P(),P(both,None,None),P(both,None),P(both,None),P(both),P(both,None,None),P(both,None),P(both),
            P(both,None),P(both,None),P(both,None),P(both))
    return jax.shard_map(functools.partial(shards,mesh.shape["gx"],mesh.shape["gy"]),mesh=mesh,in_specs=placed,
        out_specs=(P(both,None),P(both,None)),check_vma=False)
```

```python
import functools

import jax
import jax.numpy as jnp
from jax import lax
from jax.experimental import pallas as pl
from jax.experimental.pallas import tpu as pltpu
from jax.sharding import PartitionSpec as P

BOX, PB, EPS = 256, 128, 0.0025
OFFS, OP, KMAX, KP, COEF, NEAR, CAP = 316, 320, 189, 208, 121, 16, 128
ZROW = BOX + NEAR * CAP
NTAB = ZROW + 8
DROW = OFFS * BOX
LST = 3200
f32, bf16 = jnp.float32, jnp.bfloat16
AXES = ("gx", "gy")

def split3(v):
    a=v.astype(bf16).astype(f32); r=v-a
    b=r.astype(bf16).astype(f32); c=r-b
    return a,b,c

NCLS=4
LSEG=2048
NPOS=1408

def near_body(U,PU,prs_ref,own_ref,nxt_ref,out_ref,fwd_ref,xb,fa,qa,cc,dd,vv,ids,lst,num):
    sub=lax.broadcasted_iota(jnp.int32,(8,128),0)
    m3=(sub<3).astype(f32)
    one=jnp.ones((8,128),f32); zero=jnp.zeros((8,128),f32)
    for o in range(27):
        v=(o//9-1,(o//3)%3-1,o%3-1)
        vv[o]=jnp.where(sub==0,float(v[0]),jnp.where(sub==1,float(v[1]),jnp.where(sub==2,float(v[2]),0.0)))
    def rows(g,_):
        for half,ref in ((0,own_ref),(1,nxt_ref)):
            for c in range(4):
                p=ref[c,pl.ds(pl.multiple_of(g*8,8),8),:]
                if c<3: p=p-0.5
                xb[pl.ds(half*BOX*8+g*64+c,8,stride=8),:]=p
            for c in range(4,8):
                xb[pl.ds(half*BOX*8+g*64+c,8,stride=8),:]=zero
        return 0
    lax.fori_loop(0,BOX//8,rows,0)
    def feat_b(y):
        y1,y2,y3=split3(y)
        q1,q2,q3=split3(y*y)
        return jnp.concatenate([y1,y1,y1,y2,y2,y3,q1,q2,q3,one]+[zero]*6,0).astype(bf16)
    diag=lax.broadcasted_iota(jnp.int32,(PB,PB),0)==lax.broadcasted_iota(jnp.int32,(PB,PB),1)
    def sq(b):
        return xb[pl.ds(pl.multiple_of(b*8,8),8),:]
    for c in range(NCLS+1): num[c]=0
    def sort_pair(p):
        w=prs_ref[p]
        c=lax.shift_right_logical(w,22)
        k=num[c]
        lst[c*LSEG+k]=w
        num[c]=k+1
    PP=1024//(BOX//PU)//PU
    def prep(g,_):
        for u in range(PU):
            b=g*PU+u
            x=sq(b)
            x1,x2,x3=split3(x*-2.0)
            xm=x*m3
            s=jnp.sum(xm*xm,axis=0,keepdims=True)+EPS
            s=jnp.broadcast_to(s,(8,128))
            s1,s2,s3=split3(s)
            sr=jnp.where(sub==0,s1,jnp.where(sub==1,s2,jnp.where(sub==2,s3,0.0)))
            x1,x2,x3=x1*m3,x2*m3,x3*m3
            f=jnp.concatenate([x1,x2,x3,x1,x2,x1,m3,m3,m3,sr,x]+[zero]*5,0)
            t=f.T
            ft=jnp.where(lax.broadcasted_iota(jnp.int32,(PB,128),1)<80,t,0.0).astype(bf16)
            fa[b]=ft
            q=jnp.broadcast_to(t[:,83:84],(PB,PB))
            qa[b]=q
            k=lax.rsqrt(jnp.dot(ft,feat_b(x),preferred_element_type=f32))
            k=jnp.where(diag,0.0,k)
            out_ref[pl.ds(b,1),:]=jnp.sum(k*q,axis=0,keepdims=True)
            for v in range(PP): sort_pair(g*(PU*PP)+u*PP+v)
        return 0
    lax.fori_loop(0,BOX//PU,prep,0)
    def zinit(i,_):
        dd[pl.ds(pl.multiple_of(i*8,8),8),:]=zero
        cc[pl.ds(pl.multiple_of(i*8,8),8),:]=zero
        return 0
    lax.fori_loop(0,NPOS//8,zinit,0)
    ids[...]=jnp.full_like(ids,-1)
    lane1=lax.broadcasted_iota(jnp.int32,(1,128),1)
    base=jnp.int32(0)
    for cl in range(NCLS):
        R=PB//NCLS*(cl+1)
        lane=lax.broadcasted_iota(jnp.int32,(R,128),1)
        m=num[cl]
        def pairs(g,_):
            p0=base+g*U
            blk=lax.shift_right_logical(p0,7)
            l0=p0&127
            r=pl.ds(pl.multiple_of(blk*128,128),R)
            c=cc[r,:]
            ti=ids[pl.ds(blk,1),:]
            si=ids[pl.ds(16+blk,1),:]
            for u in range(U):
                ok=g*U+u<m
                pk=jnp.where(ok,lst[cl*LSEG+g*U+u],0)
                a=pk&255; b=lax.shift_right_logical(pk,8)&511; o=lax.shift_right_logical(pk,17)&31
                y=sq(b)+vv[o]
                k=lax.rsqrt(jnp.dot(fa[a,0:R,:],feat_b(y),preferred_element_type=f32))
                qb=xb[pl.ds(b*8+3,1),:]
                dd[pl.ds(p0+u,1),:]=jnp.sum(k*qa[a,0:R,:],axis=0,keepdims=True)
                c=jnp.where(lane==l0+u,jnp.sum(k*qb,axis=1,keepdims=True),c)
                ti=jnp.where(lane1==l0+u,jnp.where(ok,a,-1),ti)
                si=jnp.where(lane1==l0+u,jnp.where(ok,b,-1),si)
            cc[r,:]=c
            ids[pl.ds(blk,1),:]=ti
            ids[pl.ds(16+blk,1),:]=si
            return 0
        it=lax.div(m+U-1,U)
        lax.fori_loop(0,it,pairs,0)
        base=base+it*U
    fwd_ref[...]=jnp.zeros_like(fwd_ref)
    def scat(k,_):
        r=pl.ds(pl.multiple_of(k*128,128),128)
        oh_t=(lax.broadcasted_iota(jnp.int32,(BOX,128),0)==ids[pl.ds(k,1),:]).astype(f32).astype(bf16)
        oh_s=(lax.broadcasted_iota(jnp.int32,(2*BOX,128),0)==ids[pl.ds(16+k,1),:]).astype(f32).astype(bf16)
        c1,c2,c3=split3(cc[r,:])
        d1,d2,d3=split3(dd[r,:])
        nt=(((1,),(1,)),((),()))
        ct=sum(lax.dot_general(oh_t,c.astype(bf16),nt,preferred_element_type=f32) for c in (c1,c2,c3))
        ds=sum(jnp.dot(oh_s,d.astype(bf16),preferred_element_type=f32) for d in (d1,d2,d3))
        out_ref[...]+=ct+ds[:BOX]
        fwd_ref[...]+=ds[BOX:]
        return 0
    lax.fori_loop(0,lax.div(base+127,128),scat,0)

def pair_words(tgt,src,off,cnt,pc):
    box=jnp.arange(BOX,dtype=jnp.int32)[None,:]
    na=jnp.sum(jnp.where(tgt[:,None]==box,pc[None,:],0),1)
    nb=jnp.sum(jnp.where(src[:,None]==box,pc[None,:],0),1)
    sw=(src<BOX)&(nb<na)
    a,b,o=jnp.where(sw,src,tgt),jnp.where(sw,tgt,src),jnp.where(sw,26-off,off)
    c=(jnp.where(sw,nb,na)-1)>>5
    c=jnp.where(jnp.arange(tgt.shape[0],dtype=jnp.int32)<cnt[0],c,NCLS)
    return a+b*256+o*131072+c*4194304

def near(prs,own4,nxt4,U=128,PU=32):
    sm=pl.BlockSpec(memory_space=pltpu.SMEM); vm=pl.BlockSpec(memory_space=pltpu.VMEM)
    return pl.pallas_call(functools.partial(near_body,U,PU),
        out_shape=(jax.ShapeDtypeStruct((BOX,PB),f32),jax.ShapeDtypeStruct((BOX,PB),f32)),
        in_specs=[sm]+[vm]*2,
        out_specs=(vm,vm),
        scratch_shapes=[pltpu.VMEM((2*BOX*8,128),f32),pltpu.VMEM((BOX,PB,128),bf16),pltpu.VMEM((BOX,PB,128),f32),
            pltpu.VMEM((NPOS,128),f32),pltpu.VMEM((NPOS,128),f32),pltpu.VMEM((27,8,128),f32),pltpu.VMEM((32,128),jnp.int32),
            pltpu.SMEM(((NCLS+1)*LSEG,),jnp.int32),pltpu.SMEM((8,),jnp.int32)],
        compiler_params=pltpu.CompilerParams(vmem_limit_bytes=56<<20),
        name="near")(prs,own4,nxt4)

def swap8(rows,masks):
    rows=list(rows)
    for s,m in zip((4,2,1),masks):
        for i in range(8):
            if i&s: continue
            a,b=rows[i],rows[i+s]
            rows[i]=jnp.where(m,a,pltpu.roll(b,s,0))
            rows[i+s]=jnp.where(m,pltpu.roll(a,8-s,0),b)
    return rows

def relayout_body(in_ref,out_ref,buf):
    OB=in_ref.shape[1]
    for c in range(COEF):
        buf[c*OB:(c+1)*OB,:COEF]=in_ref[c].astype(f32)
    sub=lax.broadcasted_iota(jnp.int32,(8,128),0)
    masks=[(sub&s)==0 for s in (4,2,1)]
    for o in range(0,OB,8):
        for c in range(0,128,16):
            lo=swap8([buf[(c+i)*OB+o:(c+i)*OB+o+8,:] for i in range(8)],masks)
            hi=swap8([buf[(c+8+i)*OB+o:(c+8+i)*OB+o+8,:] for i in range(8)],masks)
            for i in range(8):
                out_ref[o+i,c:c+16,:]=jnp.concatenate([lo[i],hi[i]],0).astype(bf16)

def relayout(ops_t,OB=32):
    def outer(src,dst,buf):
        buf[...]=jnp.zeros_like(buf)
        pltpu.emit_pipeline(lambda i,o: relayout_body(i,o,buf),grid=(OP//OB,),
            in_specs=[pl.BlockSpec((COEF,OB,COEF),lambda i:(0,i,0),pipeline_mode=pl.Buffered(3))],
            out_specs=[pl.BlockSpec((OB,128,128),lambda i:(i,0,0))])(src,dst)
    hb=pl.BlockSpec(memory_space=pltpu.HBM)
    return pl.pallas_call(outer,
        out_shape=jax.ShapeDtypeStruct((OP,128,128),bf16),
        in_specs=[hb],out_specs=hb,
        scratch_shapes=[pltpu.VMEM((128*OB,128),f32)],
        compiler_params=pltpu.CompilerParams(vmem_limit_bytes=60<<20),
        name="relayout")(ops_t)

def m2l_body(U,B,OG,num_ref,want_ref,blk_ref,src_hbm,dst_hbm,lst_hbm,own_hbm,ag_hbm,ops_hbm,out_ref,
             src_ref,dst_ref,lst_ref,own_ref,ag_ref,ops,tab,tmp,dense,sem):
    T=BOX
    cps=[pltpu.make_async_copy(a,b,sem.at[i]) for i,(a,b) in enumerate(
        ((own_hbm,own_ref),(ag_hbm,ag_ref),(src_hbm,src_ref),(dst_hbm,dst_ref),(lst_hbm,lst_ref),(ops_hbm,ops)))]
    for c in cps: c.start()
    def zero(i,_):
        dense[pl.ds(pl.multiple_of(i*512,512),512),:]=jnp.zeros((512,128),f32)
        return 0
    lax.fori_loop(0,OFFS*T//512,zero,0)
    cps[0].wait()
    cps[1].wait()
    tab[0:BOX,:]=own_ref[...].astype(f32)
    tab[ZROW:ZROW+8,:]=jnp.zeros((8,128),f32)
    def reach(n,_):
        r0=pl.multiple_of(blk_ref[n]*BOX,BOX)
        tmp[...]=ag_ref[pl.ds(r0,BOX),:].astype(f32)
        d0=pl.multiple_of(BOX+n*CAP,8)
        for u in range(CAP):
            w=want_ref.at[pl.ds(u,(NEAR-1)*CAP+1)][n*CAP]
            tab[pl.ds(d0+u,1),:]=tmp[pl.ds(w,1),:]
        return 0
    lax.fori_loop(0,NEAR,reach,0)
    for c in cps[2:5]: c.wait()
    def chunk(i,_):
        for v in range(B):
            b=lst_ref.at[pl.ds(v,3072)][i*B]
            for u in range(U):
                off=(u//8)*2048+(u%8)*128
                w=pl.ds(off,KP*BOX-off)
                dense[pl.ds(dst_ref.at[w][b],1),:]=tab[pl.ds(src_ref.at[w][b],1),:]
        return 0
    lax.fori_loop(0,num_ref[0],chunk,0)
    cps[5].wait()
    out_ref[...]=jnp.zeros_like(out_ref)
    def part(o,n):
        ls=[dense[pl.ds(pl.multiple_of((o+j)*T,T),T),:].astype(bf16) for j in range(n)]
        r=ops[pl.ds(pl.multiple_of(o*128,128),n*128),:]
        out_ref[...]+=jnp.dot(jnp.concatenate(ls,1),r,preferred_element_type=f32)[:,:COEF]
    NS=OFFS//OG
    def mm(k,_):
        part(k*OG,OG)
        return 0
    lax.fori_loop(0,NS,mm,0)
    if OFFS%OG: part(NS*OG,OFFS%OG)

def m2l(src,dst,lst,num,want,blk,own,ag,ops,U=16,B=8,OG=20):
    sm=pl.BlockSpec(memory_space=pltpu.SMEM); vm=pl.BlockSpec(memory_space=pltpu.VMEM); hb=pl.BlockSpec(memory_space=pl.ANY)
    return pl.pallas_call(functools.partial(m2l_body,U,B,OG),
        out_shape=jax.ShapeDtypeStruct((BOX,COEF),f32),
        in_specs=[sm]*3+[hb]*6, out_specs=vm,
        scratch_shapes=[pltpu.SMEM((KP*BOX,),jnp.int32),pltpu.SMEM((KP*BOX,),jnp.int32),pltpu.SMEM((LST,),jnp.int32),
            pltpu.VMEM((BOX,128),bf16),pltpu.VMEM(ag.shape,bf16),pltpu.VMEM((OP*128,128),bf16),
            pltpu.VMEM((NTAB,128),f32),pltpu.VMEM((BOX,128),f32),pltpu.VMEM((DROW+8,128),f32),pltpu.SemaphoreType.DMA((6,))],
        compiler_params=pltpu.CompilerParams(vmem_limit_bytes=58<<20),
        name="m2l")(num,want,blk,src,dst,lst,own,ag,ops)

def slots(srcT,offT,cnt,U=16,B=8):
    k=lax.broadcasted_iota(jnp.int32,(KMAX,BOX),0)
    t=lax.broadcasted_iota(jnp.int32,(KMAX,BOX),1)
    s=jnp.where(k<cnt[None,:],srcT,ZROW)
    d=offT*BOX+t
    def tiled(x,fill):
        x=jnp.pad(x,((0,KP-KMAX),(0,0)),constant_values=fill)
        return x.reshape(KP//8,8,BOX//128,128).transpose(0,2,1,3).reshape(-1)
    s=tiled(s,ZROW)
    d=tiled(d,DROW)
    n=lax.div(cnt+U-1,U)
    a=jnp.arange(BOX,dtype=jnp.int32)
    incl=jnp.sum(jnp.where(a[None,:]<=a[:,None],n[None,:],0),1)
    i=jnp.arange(LST,dtype=jnp.int32)
    m=incl[None,:]<=i[:,None]
    bx=jnp.sum(m.astype(jnp.int32),1)
    c=i-jnp.sum(jnp.where(m,n[None,:],0),1)
    lst=jnp.where(bx<BOX,c*4096+(bx>>7)*1024+(bx&127),192*BOX)
    num=lax.div(jnp.sum(n)+B-1,B)
    return s,d,lst,num[None]

def ring(x,by,n):
    return lax.ppermute(x,AXES,[(i,i+by) for i in range(n) if 0<=i+by<n])

def shards(gx,gy,multipoles,m2l_ops,want_boxes,m2l_source,m2l_offset,m2l_count,positions,charges,part_count,
           pair_target,pair_source,pair_offset,pair_count):
    n=gx*gy
    x,y=lax.axis_index("gx"),lax.axis_index("gy")
    live=lax.broadcasted_iota(jnp.int32,(BOX,PB),1)<part_count[:,None]
    own4=jnp.concatenate([positions.transpose(1,0,2),jnp.where(live,charges,0.0)[None]],0)
    own=jnp.pad(multipoles,((0,0),(0,128-COEF)))
    half=gy//2
    swap=[]
    for g in range(gx):
        for j in range(gy):
            to=g+1 if j>=half else g-1
            if 0<=to<gx: swap.append((g*gy+j,to*gy+j))
    other=lax.ppermute(own,AXES,swap)
    nxt4=ring(own4,-1,n)
    other,_=lax.optimization_barrier((other,own4))
    ag=lax.all_gather(jnp.stack([own,other]),"gy").reshape(-1,128)
    me=x*gy+y
    reach=jnp.arange(NEAR,dtype=jnp.int32)
    peer=jnp.clip(me+reach-NEAR//2+(reach>=NEAR//2).astype(jnp.int32),0,n-1)
    px,py=lax.div(peer,gy),lax.rem(peer,gy)
    blk=py*2+(px!=x).astype(jnp.int32)
    s,d,lst,num=slots(m2l_source.T,m2l_offset.T,m2l_count)
    ops=relayout(m2l_ops.transpose(1,0,2)).reshape(-1,128)
    prs=pair_words(pair_target[0],pair_source[0],pair_offset[0],pair_count,part_count)
    nxt4,ops,s,d,lst,num,blk,prs=lax.optimization_barrier((nxt4,ops,s,d,lst,num,blk,prs))
    field,fwd=near(prs,own4,nxt4)
    back=ring(fwd,1,n)
    local_exp=m2l(s,d,lst,num,want_boxes.reshape(-1),blk,own,ag,ops)
    local_exp,back,field=lax.optimization_barrier((local_exp,back,field))
    return local_exp,jnp.where(live,field+back,0.0)

def solution(mesh):
    both=AXES
    placed=(P(both,None),P(),P(both,None,None),P(both,None),P(both,None),P(both),P(both,None,None),P(both,None),P(both),
            P(both,None),P(both,None),P(both,None),P(both))
    return jax.shard_map(functools.partial(shards,mesh.shape["gx"],mesh.shape["gy"]),mesh=mesh,in_specs=placed,
        out_specs=(P(both,None),P(both,None)),check_vma=False)
```

```python
import functools

import jax
import jax.numpy as jnp
from jax import lax
from jax.experimental import pallas as pl
from jax.experimental.pallas import tpu as pltpu
from jax.sharding import PartitionSpec as P

BOX, PB, EPS = 256, 128, 0.0025
OFFS, OP, KMAX, KP, COEF, NEAR, CAP = 316, 320, 189, 208, 121, 16, 128
ZROW = BOX + NEAR * CAP
NTAB = ZROW + 8
DROW = OFFS * BOX
LST = 3200
f32, bf16 = jnp.float32, jnp.bfloat16
AXES = ("gx", "gy")

def split3(v):
    a=v.astype(bf16).astype(f32); r=v-a
    b=r.astype(bf16).astype(f32); c=r-b
    return a,b,c

NCLS=4
LSEG=2048
NPOS=1408

def near_body(U,PU,prs_ref,own_ref,nxt_ref,out_ref,fwd_ref,xb,fa,qa,cc,dd,vv,ids,lst,num):
    sub=lax.broadcasted_iota(jnp.int32,(8,128),0)
    m3=(sub<3).astype(f32)
    one=jnp.ones((8,128),f32); zero=jnp.zeros((8,128),f32)
    for o in range(27):
        v=(o//9-1,(o//3)%3-1,o%3-1)
        vv[o]=jnp.where(sub==0,float(v[0]),jnp.where(sub==1,float(v[1]),jnp.where(sub==2,float(v[2]),0.0)))
    def rows(g,_):
        for half,ref in ((0,own_ref),(1,nxt_ref)):
            for c in range(4):
                p=ref[c,pl.ds(pl.multiple_of(g*8,8),8),:]
                if c<3: p=p-0.5
                xb[pl.ds(half*BOX*8+g*64+c,8,stride=8),:]=p
            for c in range(4,8):
                xb[pl.ds(half*BOX*8+g*64+c,8,stride=8),:]=zero
        return 0
    lax.fori_loop(0,BOX//8,rows,0)
    def feat_b(y):
        y1,y2,y3=split3(y)
        q1,q2,q3=split3(y*y)
        return jnp.concatenate([y1,y1,y1,y2,y2,y3,q1,q2,q3,one]+[zero]*6,0).astype(bf16)
    diag=lax.broadcasted_iota(jnp.int32,(PB,PB),0)==lax.broadcasted_iota(jnp.int32,(PB,PB),1)
    def sq(b):
        return xb[pl.ds(pl.multiple_of(b*8,8),8),:]
    for c in range(NCLS+1): num[c]=0
    def sort_pair(p):
        w=prs_ref[p]
        c=lax.shift_right_logical(w,22)
        k=num[c]
        lst[c*LSEG+k]=w
        num[c]=k+1
    PP=1024//(BOX//PU)//PU
    def prep(g,_):
        for u in range(PU):
            b=g*PU+u
            x=sq(b)
            x1,x2,x3=split3(x*-2.0)
            xm=x*m3
            s=jnp.sum(xm*xm,axis=0,keepdims=True)+EPS
            s=jnp.broadcast_to(s,(8,128))
            s1,s2,s3=split3(s)
            sr=jnp.where(sub==0,s1,jnp.where(sub==1,s2,jnp.where(sub==2,s3,0.0)))
            x1,x2,x3=x1*m3,x2*m3,x3*m3
            f=jnp.concatenate([x1,x2,x3,x1,x2,x1,m3,m3,m3,sr,x]+[zero]*5,0)
            t=f.T
            ft=jnp.where(lax.broadcasted_iota(jnp.int32,(PB,128),1)<80,t,0.0).astype(bf16)
            fa[b]=ft
            q=jnp.broadcast_to(t[:,83:84],(PB,PB))
            qa[b]=q
            k=lax.rsqrt(jnp.dot(ft,feat_b(x),preferred_element_type=f32))
            k=jnp.where(diag,0.0,k)
            out_ref[pl.ds(b,1),:]=jnp.sum(k*q,axis=0,keepdims=True)
            for v in range(PP): sort_pair(g*(PU*PP)+u*PP+v)
        return 0
    lax.fori_loop(0,BOX//PU,prep,0)
    def zinit(i,_):
        dd[pl.ds(pl.multiple_of(i*8,8),8),:]=zero
        cc[pl.ds(pl.multiple_of(i*8,8),8),:]=zero
        return 0
    lax.fori_loop(0,NPOS//8,zinit,0)
    ids[...]=jnp.full_like(ids,-1)
    lane1=lax.broadcasted_iota(jnp.int32,(1,128),1)
    base=jnp.int32(0)
    for cl in range(NCLS):
        R=PB//NCLS*(cl+1)
        lane=lax.broadcasted_iota(jnp.int32,(R,128),1)
        m=num[cl]
        def pairs(g,_):
            p0=base+g*U
            blk=lax.shift_right_logical(p0,7)
            l0=p0&127
            r=pl.ds(pl.multiple_of(blk*128,128),R)
            c=cc[r,:]
            ti=ids[pl.ds(blk,1),:]
            si=ids[pl.ds(16+blk,1),:]
            for u in range(U):
                ok=g*U+u<m
                pk=jnp.where(ok,lst[cl*LSEG+g*U+u],0)
                a=pk&255; b=lax.shift_right_logical(pk,8)&511; o=lax.shift_right_logical(pk,17)&31
                y=sq(b)+vv[o]
                k=lax.rsqrt(jnp.dot(fa[a,0:R,:],feat_b(y),preferred_element_type=f32))
                qb=xb[pl.ds(b*8+3,1),:]
                dd[pl.ds(p0+u,1),:]=jnp.sum(k*qa[a,0:R,:],axis=0,keepdims=True)
                c=jnp.where(lane==l0+u,jnp.sum(k*qb,axis=1,keepdims=True),c)
                ti=jnp.where(lane1==l0+u,jnp.where(ok,a,-1),ti)
                si=jnp.where(lane1==l0+u,jnp.where(ok,b,-1),si)
            cc[r,:]=c
            ids[pl.ds(blk,1),:]=ti
            ids[pl.ds(16+blk,1),:]=si
            return 0
        it=lax.div(m+U-1,U)
        lax.fori_loop(0,it,pairs,0)
        base=base+it*U
    fwd_ref[...]=jnp.zeros_like(fwd_ref)
    def scat(k,_):
        r=pl.ds(pl.multiple_of(k*128,128),128)
        oh_t=(lax.broadcasted_iota(jnp.int32,(BOX,128),0)==ids[pl.ds(k,1),:]).astype(f32).astype(bf16)
        oh_s=(lax.broadcasted_iota(jnp.int32,(2*BOX,128),0)==ids[pl.ds(16+k,1),:]).astype(f32).astype(bf16)
        c1,c2,c3=split3(cc[r,:])
        d1,d2,d3=split3(dd[r,:])
        nt=(((1,),(1,)),((),()))
        ct=sum(lax.dot_general(oh_t,c.astype(bf16),nt,preferred_element_type=f32) for c in (c1,c2,c3))
        ds=sum(jnp.dot(oh_s,d.astype(bf16),preferred_element_type=f32) for d in (d1,d2,d3))
        out_ref[...]+=ct+ds[:BOX]
        fwd_ref[...]+=ds[BOX:]
        return 0
    lax.fori_loop(0,lax.div(base+127,128),scat,0)

def pair_words(tgt,src,off,cnt,pc):
    box=jnp.arange(BOX,dtype=jnp.int32)[None,:]
    na=jnp.sum(jnp.where(tgt[:,None]==box,pc[None,:],0),1)
    nb=jnp.sum(jnp.where(src[:,None]==box,pc[None,:],0),1)
    sw=(src<BOX)&(nb<na)
    a,b,o=jnp.where(sw,src,tgt),jnp.where(sw,tgt,src),jnp.where(sw,26-off,off)
    c=(jnp.where(sw,nb,na)-1)>>5
    c=jnp.where(jnp.arange(tgt.shape[0],dtype=jnp.int32)<cnt[0],c,NCLS)
    return a+b*256+o*131072+c*4194304

def near(prs,own4,nxt4,U=128,PU=32):
    sm=pl.BlockSpec(memory_space=pltpu.SMEM); vm=pl.BlockSpec(memory_space=pltpu.VMEM)
    return pl.pallas_call(functools.partial(near_body,U,PU),
        out_shape=(jax.ShapeDtypeStruct((BOX,PB),f32),jax.ShapeDtypeStruct((BOX,PB),f32)),
        in_specs=[sm]+[vm]*2,
        out_specs=(vm,vm),
        scratch_shapes=[pltpu.VMEM((2*BOX*8,128),f32),pltpu.VMEM((BOX,PB,128),bf16),pltpu.VMEM((BOX,PB,128),f32),
            pltpu.VMEM((NPOS,128),f32),pltpu.VMEM((NPOS,128),f32),pltpu.VMEM((27,8,128),f32),pltpu.VMEM((32,128),jnp.int32),
            pltpu.SMEM(((NCLS+1)*LSEG,),jnp.int32),pltpu.SMEM((8,),jnp.int32)],
        compiler_params=pltpu.CompilerParams(vmem_limit_bytes=62<<20),
        name="near")(prs,own4,nxt4)

def swap8(rows,masks):
    rows=list(rows)
    for s,m in zip((4,2,1),masks):
        for i in range(8):
            if i&s: continue
            a,b=rows[i],rows[i+s]
            rows[i]=jnp.where(m,a,pltpu.roll(b,s,0))
            rows[i+s]=jnp.where(m,pltpu.roll(a,8-s,0),b)
    return rows

def relayout_body(in_ref,out_ref,buf):
    OB=in_ref.shape[1]
    for c in range(COEF):
        buf[c*OB:(c+1)*OB,:COEF]=in_ref[c].astype(f32)
    sub=lax.broadcasted_iota(jnp.int32,(8,128),0)
    masks=[(sub&s)==0 for s in (4,2,1)]
    for o in range(0,OB,8):
        for c in range(0,128,16):
            lo=swap8([buf[(c+i)*OB+o:(c+i)*OB+o+8,:] for i in range(8)],masks)
            hi=swap8([buf[(c+8+i)*OB+o:(c+8+i)*OB+o+8,:] for i in range(8)],masks)
            for i in range(8):
                out_ref[o+i,c:c+16,:]=jnp.concatenate([lo[i],hi[i]],0).astype(bf16)

def relayout(ops_t,OB=32):
    def outer(src,dst,buf):
        buf[...]=jnp.zeros_like(buf)
        pltpu.emit_pipeline(lambda i,o: relayout_body(i,o,buf),grid=(OP//OB,),
            in_specs=[pl.BlockSpec((COEF,OB,COEF),lambda i:(0,i,0),pipeline_mode=pl.Buffered(3))],
            out_specs=[pl.BlockSpec((OB,128,128),lambda i:(i,0,0))])(src,dst)
    hb=pl.BlockSpec(memory_space=pltpu.HBM)
    return pl.pallas_call(outer,
        out_shape=jax.ShapeDtypeStruct((OP,128,128),bf16),
        in_specs=[hb],out_specs=hb,
        scratch_shapes=[pltpu.VMEM((128*OB,128),f32)],
        compiler_params=pltpu.CompilerParams(vmem_limit_bytes=60<<20),
        name="relayout")(ops_t)

def m2l_body(U,B,OG,num_ref,want_ref,src_hbm,dst_hbm,lst_hbm,own_hbm,p0_hbm,p1_hbm,p2_hbm,p3_hbm,ops_hbm,out_ref,
             src_ref,dst_ref,lst_ref,own_ref,ag_ref,ops,tab,tmp,dense,sem):
    T=BOX
    cps=[pltpu.make_async_copy(a,b,sem.at[i]) for i,(a,b) in enumerate(
        [(own_hbm,own_ref),(src_hbm,src_ref),(dst_hbm,dst_ref),(lst_hbm,lst_ref),(ops_hbm,ops)]
        +[(p,ag_ref.at[pl.ds(k*4*BOX,4*BOX),:]) for k,p in enumerate((p0_hbm,p1_hbm,p2_hbm,p3_hbm))])]
    for c in cps: c.start()
    def zero(i,_):
        dense[pl.ds(pl.multiple_of(i*512,512),512),:]=jnp.zeros((512,128),f32)
        return 0
    lax.fori_loop(0,OFFS*T//512,zero,0)
    cps[0].wait()
    for c in cps[5:]: c.wait()
    tab[0:BOX,:]=own_ref[...].astype(f32)
    tab[ZROW:ZROW+8,:]=jnp.zeros((8,128),f32)
    def reach(n,_):
        r0=pl.multiple_of(n*BOX,BOX)
        tmp[...]=ag_ref[pl.ds(r0,BOX),:].astype(f32)
        d0=pl.multiple_of(BOX+n*CAP,8)
        for u in range(CAP):
            w=want_ref.at[pl.ds(u,(NEAR-1)*CAP+1)][n*CAP]
            tab[pl.ds(d0+u,1),:]=tmp[pl.ds(w,1),:]
        return 0
    lax.fori_loop(0,NEAR,reach,0)
    for c in cps[1:4]: c.wait()
    def chunk(i,_):
        for v in range(B):
            b=lst_ref.at[pl.ds(v,3072)][i*B]
            for u in range(U):
                off=(u//8)*2048+(u%8)*128
                w=pl.ds(off,KP*BOX-off)
                dense[pl.ds(dst_ref.at[w][b],1),:]=tab[pl.ds(src_ref.at[w][b],1),:]
        return 0
    lax.fori_loop(0,num_ref[0],chunk,0)
    cps[4].wait()
    out_ref[...]=jnp.zeros_like(out_ref)
    def part(o,n):
        ls=[dense[pl.ds(pl.multiple_of((o+j)*T,T),T),:].astype(bf16) for j in range(n)]
        r=ops[pl.ds(pl.multiple_of(o*128,128),n*128),:]
        out_ref[...]+=jnp.dot(jnp.concatenate(ls,1),r,preferred_element_type=f32)[:,:COEF]
    NS=OFFS//OG
    def mm(k,_):
        part(k*OG,OG)
        return 0
    lax.fori_loop(0,NS,mm,0)
    if OFFS%OG: part(NS*OG,OFFS%OG)

def m2l(src,dst,lst,num,want,own,p0,p1,p2,p3,ops,U=16,B=8,OG=20):
    sm=pl.BlockSpec(memory_space=pltpu.SMEM); vm=pl.BlockSpec(memory_space=pltpu.VMEM); hb=pl.BlockSpec(memory_space=pl.ANY)
    return pl.pallas_call(functools.partial(m2l_body,U,B,OG),
        out_shape=jax.ShapeDtypeStruct((BOX,COEF),f32),
        in_specs=[sm]*2+[hb]*9, out_specs=vm,
        scratch_shapes=[pltpu.SMEM((KP*BOX,),jnp.int32),pltpu.SMEM((KP*BOX,),jnp.int32),pltpu.SMEM((LST,),jnp.int32),
            pltpu.VMEM((BOX,128),bf16),pltpu.VMEM((NEAR*BOX,128),bf16),pltpu.VMEM((OP*128,128),bf16),
            pltpu.VMEM((NTAB,128),f32),pltpu.VMEM((BOX,128),f32),pltpu.VMEM((DROW+8,128),f32),pltpu.SemaphoreType.DMA((9,))],
        compiler_params=pltpu.CompilerParams(vmem_limit_bytes=58<<20),
        name="m2l")(num,want,src,dst,lst,own,p0,p1,p2,p3,ops)

def slots(srcT,offT,cnt,U=16,B=8):
    k=lax.broadcasted_iota(jnp.int32,(KMAX,BOX),0)
    t=lax.broadcasted_iota(jnp.int32,(KMAX,BOX),1)
    s=jnp.where(k<cnt[None,:],srcT,ZROW)
    d=offT*BOX+t
    def tiled(x,fill):
        x=jnp.pad(x,((0,KP-KMAX),(0,0)),constant_values=fill)
        return x.reshape(KP//8,8,BOX//128,128).transpose(0,2,1,3).reshape(-1)
    s=tiled(s,ZROW)
    d=tiled(d,DROW)
    n=lax.div(cnt+U-1,U)
    a=jnp.arange(BOX,dtype=jnp.int32)
    incl=jnp.sum(jnp.where(a[None,:]<=a[:,None],n[None,:],0),1)
    i=jnp.arange(LST,dtype=jnp.int32)
    m=incl[None,:]<=i[:,None]
    bx=jnp.sum(m.astype(jnp.int32),1)
    c=i-jnp.sum(jnp.where(m,n[None,:],0),1)
    lst=jnp.where(bx<BOX,c*4096+(bx>>7)*1024+(bx&127),192*BOX)
    num=lax.div(jnp.sum(n)+B-1,B)
    return s,d,lst,num[None]

def ring(x,by,n):
    return lax.ppermute(x,AXES,[(i,i+by) for i in range(n) if 0<=i+by<n])

def around(x,by,n):
    return lax.ppermute(x,AXES,[(i,(i+by)%n) for i in range(n)])

def shards(gx,gy,multipoles,m2l_ops,want_boxes,m2l_source,m2l_offset,m2l_count,positions,charges,part_count,
           pair_target,pair_source,pair_offset,pair_count):
    n=gx*gy
    live=lax.broadcasted_iota(jnp.int32,(BOX,PB),1)<part_count[:,None]
    own4=jnp.concatenate([positions.transpose(1,0,2),jnp.where(live,charges,0.0)[None]],0)
    own=jnp.pad(multipoles,((0,0),(0,128-COEF)))
    a1,b1=around(own,1,n),around(own,-1,n)
    a1,b1,own4=lax.optimization_barrier((a1,b1,own4))
    three=jnp.concatenate([a1,own,b1])
    a3,b3=around(three,3,n),around(three,-3,n)
    nxt4=ring(own4,-1,n)
    s,d,lst,num=slots(m2l_source.T,m2l_offset.T,m2l_count)
    ops=relayout(m2l_ops.transpose(1,0,2)).reshape(-1,128)
    prs=pair_words(pair_target[0],pair_source[0],pair_offset[0],pair_count,part_count)
    low,high=jnp.concatenate([a3,a1]),jnp.concatenate([b1,b3])
    nxt4,ops,s,d,lst,num,prs,low,high=lax.optimization_barrier((nxt4,ops,s,d,lst,num,prs,low,high))
    a4,b4=around(low,4,n),around(high,-4,n)
    field,fwd=near(prs,own4,nxt4)
    back=ring(fwd,1,n)
    local_exp=m2l(s,d,lst,num,want_boxes.reshape(-1),own,a4,low,high,b4,ops)
    local_exp,back,field=lax.optimization_barrier((local_exp,back,field))
    return local_exp,jnp.where(live,field+back,0.0)

def solution(mesh):
    both=AXES
    placed=(P(both,None),P(),P(both,None,None),P(both,None),P(both,None),P(both),P(both,None,None),P(both,None),P(both),
            P(both,None),P(both,None),P(both,None),P(both))
    return jax.shard_map(functools.partial(shards,mesh.shape["gx"],mesh.shape["gy"]),mesh=mesh,in_specs=placed,
        out_specs=(P(both,None),P(both,None)),check_vma=False)
```

```python
import functools

import jax
import jax.numpy as jnp
from jax import lax
from jax.experimental import pallas as pl
from jax.experimental.pallas import tpu as pltpu
from jax.sharding import PartitionSpec as P

BOX, PB, EPS = 256, 128, 0.0025
OFFS, OP, KMAX, KP, COEF, NEAR, CAP = 316, 320, 189, 208, 121, 16, 128
ZROW = BOX + NEAR * CAP
NTAB = ZROW + 8
DROW = OFFS * BOX
LST = 3200
f32, bf16 = jnp.float32, jnp.bfloat16
AXES = ("gx", "gy")

def split3(v):
    a=v.astype(bf16).astype(f32); r=v-a
    b=r.astype(bf16).astype(f32); c=r-b
    return a,b,c

NCLS=4
LSEG=2048
NPOS=1408

def near_body(U,PU,prs_ref,own_ref,nxt_ref,out_ref,fwd_ref,xb,fa,qa,cc,dd,vv,ids,lst,num):
    sub=lax.broadcasted_iota(jnp.int32,(8,128),0)
    m3=(sub<3).astype(f32)
    one=jnp.ones((8,128),f32); zero=jnp.zeros((8,128),f32)
    for o in range(27):
        v=(o//9-1,(o//3)%3-1,o%3-1)
        vv[o]=jnp.where(sub==0,float(v[0]),jnp.where(sub==1,float(v[1]),jnp.where(sub==2,float(v[2]),0.0)))
    def rows(g,_):
        for half,ref in ((0,own_ref),(1,nxt_ref)):
            for c in range(4):
                p=ref[c,pl.ds(pl.multiple_of(g*8,8),8),:]
                if c<3: p=p-0.5
                xb[pl.ds(half*BOX*8+g*64+c,8,stride=8),:]=p
            for c in range(4,8):
                xb[pl.ds(half*BOX*8+g*64+c,8,stride=8),:]=zero
        return 0
    lax.fori_loop(0,BOX//8,rows,0)
    def feat_b(y):
        y1,y2,y3=split3(y)
        q1,q2,q3=split3(y*y)
        return jnp.concatenate([y1,y1,y1,y2,y2,y3,q1,q2,q3,one]+[zero]*6,0).astype(bf16)
    diag=lax.broadcasted_iota(jnp.int32,(PB,PB),0)==lax.broadcasted_iota(jnp.int32,(PB,PB),1)
    def sq(b):
        return xb[pl.ds(pl.multiple_of(b*8,8),8),:]
    for c in range(NCLS+1): num[c]=0
    def sort_pair(p):
        w=prs_ref[p]
        c=lax.shift_right_logical(w,22)
        k=num[c]
        lst[c*LSEG+k]=w
        num[c]=k+1
    PP=1024//(BOX//PU)//PU
    def prep(g,_):
        for u in range(PU):
            b=g*PU+u
            x=sq(b)
            x1,x2,x3=split3(x*-2.0)
            xm=x*m3
            s=jnp.sum(xm*xm,axis=0,keepdims=True)+EPS
            s=jnp.broadcast_to(s,(8,128))
            s1,s2,s3=split3(s)
            sr=jnp.where(sub==0,s1,jnp.where(sub==1,s2,jnp.where(sub==2,s3,0.0)))
            x1,x2,x3=x1*m3,x2*m3,x3*m3
            f=jnp.concatenate([x1,x2,x3,x1,x2,x1,m3,m3,m3,sr,x]+[zero]*5,0)
            t=f.T
            ft=jnp.where(lax.broadcasted_iota(jnp.int32,(PB,128),1)<80,t,0.0).astype(bf16)
            fa[b]=ft
            q=jnp.broadcast_to(t[:,83:84],(PB,PB))
            qa[b]=q
            k=lax.rsqrt(jnp.dot(ft,feat_b(x),preferred_element_type=f32))
            k=jnp.where(diag,0.0,k)
            out_ref[pl.ds(b,1),:]=jnp.sum(k*q,axis=0,keepdims=True)
            for v in range(PP): sort_pair(g*(PU*PP)+u*PP+v)
        return 0
    lax.fori_loop(0,BOX//PU,prep,0)
    def zinit(i,_):
        dd[pl.ds(pl.multiple_of(i*8,8),8),:]=zero
        cc[pl.ds(pl.multiple_of(i*8,8),8),:]=zero
        return 0
    lax.fori_loop(0,NPOS//8,zinit,0)
    ids[...]=jnp.full_like(ids,-1)
    lane1=lax.broadcasted_iota(jnp.int32,(1,128),1)
    base=jnp.int32(0)
    for cl in range(NCLS):
        R=PB//NCLS*(cl+1)
        lane=lax.broadcasted_iota(jnp.int32,(R,128),1)
        m=num[cl]
        def pairs(g,_):
            p0=base+g*U
            blk=lax.shift_right_logical(p0,7)
            l0=p0&127
            r=pl.ds(pl.multiple_of(blk*128,128),R)
            c=cc[r,:]
            ti=ids[pl.ds(blk,1),:]
            si=ids[pl.ds(16+blk,1),:]
            for u in range(U):
                ok=g*U+u<m
                pk=jnp.where(ok,lst[cl*LSEG+g*U+u],0)
                a=pk&255; b=lax.shift_right_logical(pk,8)&511; o=lax.shift_right_logical(pk,17)&31
                y=sq(b)+vv[o]
                k=lax.rsqrt(jnp.dot(fa[a,0:R,:],feat_b(y),preferred_element_type=f32))
                qb=xb[pl.ds(b*8+3,1),:]
                dd[pl.ds(p0+u,1),:]=jnp.sum(k*qa[a,0:R,:],axis=0,keepdims=True)
                c=jnp.where(lane==l0+u,jnp.sum(k*qb,axis=1,keepdims=True),c)
                ti=jnp.where(lane1==l0+u,jnp.where(ok,a,-1),ti)
                si=jnp.where(lane1==l0+u,jnp.where(ok,b,-1),si)
            cc[r,:]=c
            ids[pl.ds(blk,1),:]=ti
            ids[pl.ds(16+blk,1),:]=si
            return 0
        it=lax.div(m+U-1,U)
        lax.fori_loop(0,it,pairs,0)
        base=base+it*U
    fwd_ref[...]=jnp.zeros_like(fwd_ref)
    def scat(k,_):
        r=pl.ds(pl.multiple_of(k*128,128),128)
        oh_t=(lax.broadcasted_iota(jnp.int32,(BOX,128),0)==ids[pl.ds(k,1),:]).astype(f32).astype(bf16)
        oh_s=(lax.broadcasted_iota(jnp.int32,(2*BOX,128),0)==ids[pl.ds(16+k,1),:]).astype(f32).astype(bf16)
        c1,c2,c3=split3(cc[r,:])
        d1,d2,d3=split3(dd[r,:])
        nt=(((1,),(1,)),((),()))
        ct=sum(lax.dot_general(oh_t,c.astype(bf16),nt,preferred_element_type=f32) for c in (c1,c2,c3))
        ds=sum(jnp.dot(oh_s,d.astype(bf16),preferred_element_type=f32) for d in (d1,d2,d3))
        out_ref[...]+=ct+ds[:BOX]
        fwd_ref[...]+=ds[BOX:]
        return 0
    lax.fori_loop(0,lax.div(base+127,128),scat,0)

def pair_words(tgt,src,off,cnt,pc):
    box=jnp.arange(BOX,dtype=jnp.int32)[None,:]
    na=jnp.sum(jnp.where(tgt[:,None]==box,pc[None,:],0),1)
    nb=jnp.sum(jnp.where(src[:,None]==box,pc[None,:],0),1)
    sw=(src<BOX)&(nb<na)
    a,b,o=jnp.where(sw,src,tgt),jnp.where(sw,tgt,src),jnp.where(sw,26-off,off)
    c=(jnp.where(sw,nb,na)-1)>>5
    c=jnp.where(jnp.arange(tgt.shape[0],dtype=jnp.int32)<cnt[0],c,NCLS)
    return a+b*256+o*131072+c*4194304

def near(prs,own4,nxt4,U=128,PU=64):
    sm=pl.BlockSpec(memory_space=pltpu.SMEM); vm=pl.BlockSpec(memory_space=pltpu.VMEM)
    return pl.pallas_call(functools.partial(near_body,U,PU),
        out_shape=(jax.ShapeDtypeStruct((BOX,PB),f32),jax.ShapeDtypeStruct((BOX,PB),f32)),
        in_specs=[sm]+[vm]*2,
        out_specs=(vm,vm),
        scratch_shapes=[pltpu.VMEM((2*BOX*8,128),f32),pltpu.VMEM((BOX,PB,128),bf16),pltpu.VMEM((BOX,PB,128),f32),
            pltpu.VMEM((NPOS,128),f32),pltpu.VMEM((NPOS,128),f32),pltpu.VMEM((27,8,128),f32),pltpu.VMEM((32,128),jnp.int32),
            pltpu.SMEM(((NCLS+1)*LSEG,),jnp.int32),pltpu.SMEM((8,),jnp.int32)],
        compiler_params=pltpu.CompilerParams(vmem_limit_bytes=62<<20),
        name="near")(prs,own4,nxt4)

def swap8(rows,masks):
    rows=list(rows)
    for s,m in zip((4,2,1),masks):
        for i in range(8):
            if i&s: continue
            a,b=rows[i],rows[i+s]
            rows[i]=jnp.where(m,a,pltpu.roll(b,s,0))
            rows[i+s]=jnp.where(m,pltpu.roll(a,8-s,0),b)
    return rows

def relayout_body(in_ref,out_ref,buf):
    OB=in_ref.shape[1]
    for c in range(COEF):
        buf[c*OB:(c+1)*OB,:COEF]=in_ref[c].astype(f32)
    sub=lax.broadcasted_iota(jnp.int32,(8,128),0)
    masks=[(sub&s)==0 for s in (4,2,1)]
    for o in range(0,OB,8):
        for c in range(0,128,16):
            lo=swap8([buf[(c+i)*OB+o:(c+i)*OB+o+8,:] for i in range(8)],masks)
            hi=swap8([buf[(c+8+i)*OB+o:(c+8+i)*OB+o+8,:] for i in range(8)],masks)
            for i in range(8):
                out_ref[o+i,c:c+16,:]=jnp.concatenate([lo[i],hi[i]],0).astype(bf16)

def relayout(ops_t,OB=32):
    def outer(src,dst,buf):
        buf[...]=jnp.zeros_like(buf)
        pltpu.emit_pipeline(lambda i,o: relayout_body(i,o,buf),grid=(OP//OB,),
            in_specs=[pl.BlockSpec((COEF,OB,COEF),lambda i:(0,i,0),pipeline_mode=pl.Buffered(3))],
            out_specs=[pl.BlockSpec((OB,128,128),lambda i:(i,0,0))])(src,dst)
    hb=pl.BlockSpec(memory_space=pltpu.HBM)
    return pl.pallas_call(outer,
        out_shape=jax.ShapeDtypeStruct((OP,128,128),bf16),
        in_specs=[hb],out_specs=hb,
        scratch_shapes=[pltpu.VMEM((128*OB,128),f32)],
        compiler_params=pltpu.CompilerParams(vmem_limit_bytes=60<<20),
        name="relayout")(ops_t)

def m2l_body(U,B,OG,num_ref,want_ref,blk_ref,src_hbm,dst_hbm,lst_hbm,own_hbm,ag_hbm,ops_hbm,out_ref,
             src_ref,dst_ref,lst_ref,own_ref,ag_ref,ops,tab,tmp,dense,sem):
    T=BOX
    cps=[pltpu.make_async_copy(a,b,sem.at[i]) for i,(a,b) in enumerate(
        ((own_hbm,own_ref),(ag_hbm,ag_ref),(src_hbm,src_ref),(dst_hbm,dst_ref),(lst_hbm,lst_ref),(ops_hbm,ops)))]
    for c in cps: c.start()
    def zero(i,_):
        dense[pl.ds(pl.multiple_of(i*512,512),512),:]=jnp.zeros((512,128),f32)
        return 0
    lax.fori_loop(0,OFFS*T//512,zero,0)
    cps[0].wait()
    cps[1].wait()
    tab[0:BOX,:]=own_ref[...].astype(f32)
    tab[ZROW:ZROW+8,:]=jnp.zeros((8,128),f32)
    def reach(n,_):
        r0=pl.multiple_of(blk_ref[n]*BOX,BOX)
        tmp[...]=ag_ref[pl.ds(r0,BOX),:].astype(f32)
        d0=pl.multiple_of(BOX+n*CAP,8)
        for u in range(CAP):
            w=want_ref.at[pl.ds(u,(NEAR-1)*CAP+1)][n*CAP]
            tab[pl.ds(d0+u,1),:]=tmp[pl.ds(w,1),:]
        return 0
    lax.fori_loop(0,NEAR,reach,0)
    for c in cps[2:5]: c.wait()
    def chunk(i,_):
        for v in range(B):
            b=lst_ref.at[pl.ds(v,3072)][i*B]
            for u in range(U):
                off=(u//8)*2048+(u%8)*128
                w=pl.ds(off,KP*BOX-off)
                dense[pl.ds(dst_ref.at[w][b],1),:]=tab[pl.ds(src_ref.at[w][b],1),:]
        return 0
    lax.fori_loop(0,num_ref[0],chunk,0)
    cps[5].wait()
    out_ref[...]=jnp.zeros_like(out_ref)
    def part(o,n):
        ls=[dense[pl.ds(pl.multiple_of((o+j)*T,T),T),:].astype(bf16) for j in range(n)]
        r=ops[pl.ds(pl.multiple_of(o*128,128),n*128),:]
        out_ref[...]+=jnp.dot(jnp.concatenate(ls,1),r,preferred_element_type=f32)[:,:COEF]
    NS=OFFS//OG
    def mm(k,_):
        part(k*OG,OG)
        return 0
    lax.fori_loop(0,NS,mm,0)
    if OFFS%OG: part(NS*OG,OFFS%OG)

def m2l(src,dst,lst,num,want,blk,own,ag,ops,U=16,B=16,OG=20):
    sm=pl.BlockSpec(memory_space=pltpu.SMEM); vm=pl.BlockSpec(memory_space=pltpu.VMEM); hb=pl.BlockSpec(memory_space=pl.ANY)
    return pl.pallas_call(functools.partial(m2l_body,U,B,OG),
        out_shape=jax.ShapeDtypeStruct((BOX,COEF),f32),
        in_specs=[sm]*3+[hb]*6, out_specs=vm,
        scratch_shapes=[pltpu.SMEM((KP*BOX,),jnp.int32),pltpu.SMEM((KP*BOX,),jnp.int32),pltpu.SMEM((LST,),jnp.int32),
            pltpu.VMEM((BOX,128),bf16),pltpu.VMEM(ag.shape,bf16),pltpu.VMEM((OP*128,128),bf16),
            pltpu.VMEM((NTAB,128),f32),pltpu.VMEM((BOX,128),f32),pltpu.VMEM((DROW+8,128),f32),pltpu.SemaphoreType.DMA((6,))],
        compiler_params=pltpu.CompilerParams(vmem_limit_bytes=58<<20),
        name="m2l")(num,want,blk,src,dst,lst,own,ag,ops)

def slots(srcT,offT,cnt,U=16,B=16):
    k=lax.broadcasted_iota(jnp.int32,(KMAX,BOX),0)
    t=lax.broadcasted_iota(jnp.int32,(KMAX,BOX),1)
    s=jnp.where(k<cnt[None,:],srcT,ZROW)
    d=offT*BOX+t
    def tiled(x,fill):
        x=jnp.pad(x,((0,KP-KMAX),(0,0)),constant_values=fill)
        return x.reshape(KP//8,8,BOX//128,128).transpose(0,2,1,3).reshape(-1)
    s=tiled(s,ZROW)
    d=tiled(d,DROW)
    n=lax.div(cnt+U-1,U)
    a=jnp.arange(BOX,dtype=jnp.int32)
    incl=jnp.sum(jnp.where(a[None,:]<=a[:,None],n[None,:],0),1)
    i=jnp.arange(LST,dtype=jnp.int32)
    m=incl[None,:]<=i[:,None]
    bx=jnp.sum(m.astype(jnp.int32),1)
    c=i-jnp.sum(jnp.where(m,n[None,:],0),1)
    lst=jnp.where(bx<BOX,c*4096+(bx>>7)*1024+(bx&127),192*BOX)
    num=lax.div(jnp.sum(n)+B-1,B)
    return s,d,lst,num[None]

def ring(x,by,n):
    return lax.ppermute(x,AXES,[(i,i+by) for i in range(n) if 0<=i+by<n])

def shards(gx,gy,multipoles,m2l_ops,want_boxes,m2l_source,m2l_offset,m2l_count,positions,charges,part_count,
           pair_target,pair_source,pair_offset,pair_count):
    n=gx*gy
    x,y=lax.axis_index("gx"),lax.axis_index("gy")
    live=lax.broadcasted_iota(jnp.int32,(BOX,PB),1)<part_count[:,None]
    own4=jnp.concatenate([positions.transpose(1,0,2),jnp.where(live,charges,0.0)[None]],0)
    own=jnp.pad(multipoles,((0,0),(0,128-COEF)))
    half=gy//2
    swap=[]
    for g in range(gx):
        for j in range(gy):
            to=g+1 if j>=half else g-1
            if 0<=to<gx: swap.append((g*gy+j,to*gy+j))
    other=lax.ppermute(own,AXES,swap)
    nxt4=ring(own4,-1,n)
    other,_=lax.optimization_barrier((other,own4))
    ag=lax.all_gather(jnp.stack([own,other]),"gy").reshape(-1,128)
    me=x*gy+y
    reach=jnp.arange(NEAR,dtype=jnp.int32)
    peer=jnp.clip(me+reach-NEAR//2+(reach>=NEAR//2).astype(jnp.int32),0,n-1)
    px,py=lax.div(peer,gy),lax.rem(peer,gy)
    blk=py*2+(px!=x).astype(jnp.int32)
    s,d,lst,num=slots(m2l_source.T,m2l_offset.T,m2l_count)
    ops=relayout(m2l_ops.transpose(1,0,2)).reshape(-1,128)
    prs=pair_words(pair_target[0],pair_source[0],pair_offset[0],pair_count,part_count)
    nxt4,ops,s,d,lst,num,blk,prs=lax.optimization_barrier((nxt4,ops,s,d,lst,num,blk,prs))
    field,fwd=near(prs,own4,nxt4)
    back=ring(fwd,1,n)
    local_exp=m2l(s,d,lst,num,want_boxes.reshape(-1),blk,own,ag,ops)
    local_exp,back,field=lax.optimization_barrier((local_exp,back,field))
    return local_exp,jnp.where(live,field+back,0.0)

def solution(mesh):
    both=AXES
    placed=(P(both,None),P(),P(both,None,None),P(both,None),P(both,None),P(both),P(both,None,None),P(both,None),P(both),
            P(both,None),P(both,None),P(both,None),P(both))
    return jax.shard_map(functools.partial(shards,mesh.shape["gx"],mesh.shape["gy"]),mesh=mesh,in_specs=placed,
        out_specs=(P(both,None),P(both,None)),check_vma=False)
```
